128 devices in a mesh: section: 16 (over x, z), expert: 8 (over y, core).
Axes of the slice: x: 4, y: 4, z: 4, core: 2. Of those that a mesh axis runs over, the one named last changes fastest.
Arguments:
- tokens: bfloat16 [2048, 4096], P(('section', 'expert')), may hold values from -6 to 6
- routes: int32 [2048, 2], P(('section', 'expert')), may hold values from 0 to 7, all different within a row; in each aligned block of 16 rows (0 to 15, 16 to 31, ...) at most 8 rows name the same one
- router_weight: bfloat16 [4096, 8], replicated, may hold values from -0.09375 to 0.09375
- gate_weight: bfloat16 [8, 4096, 14336], P('expert', None, 'section'), may hold values from -0.09375 to 0.09375
- up_weight: bfloat16 [8, 4096, 14336], P('expert', None, 'section'), may hold values from -0.09375 to 0.09375
- down_weight: bfloat16 [8, 14336, 4096], P('expert', 'section'), may hold values from -0.046875 to 0.046875
Outputs:
- mixed: bfloat16 [2048, 4096], P(('section', 'expert'))
The draws below stay inside these ranges and needn't reach their ends.
Inputs may be any that keep to these rules, and one draw needn't show every extreme that they name: `routes`: each token names two different experts; the 16 tokens of one device name one expert at most 8 times, and in every draw some device's tokens name some expert exactly 8 times.
All inputs are finite; a program needn't handle non-finite values.
Results may differ from the reference program's by a relative error of at most 0.024.
Values may be sent and summed in bfloat16 or wider, within the bound.
A program may use at most 128 MiB of HBM per device.

```python
import math
import jax
import jax.numpy as jnp
import numpy as np
from jax import lax

D = 4096
TOP = 2
FF_DEV = 896
FF = 14336
EXPERTS = 8
TOK_DEV = 16
CAP = 8
TOKENS = 2048
N_SECTION = 16


def steps_of(own_key, extent, split, least, top_value):
    loudness, own = 1.0, jax.random.fold_in(own_key, 6)
    for position, blocks in split:
        steps = jnp.exp(jax.random.uniform(jax.random.fold_in(own, position), (blocks,), jnp.float32, least / len(split), top_value / len(split)))
        loudness = loudness * jnp.repeat(steps, extent[position] // blocks).reshape([-1 if axis == position else 1 for axis in range(len(extent))])
    return loudness


def routed_block(key, own, number, rows, amount, top, reach, lean):
    sequence = jax.random.permutation(key, amount)
    heavy_load, ordinary = shares(amount, rows * top, reach, lean, True), shares(amount, rows * top, reach, lean, False)
    places = jnp.arange(amount)

    def named(lengths, turn):
        used = int((lengths > 0).sum())
        fixed = max(1, used // 4)
        passed = fixed + (places - fixed + turn * (used - fixed)) % max(1, amount - fixed)
        return jnp.zeros((amount,), jnp.int32).at[sequence[jnp.where(places < fixed, places, passed)]].set(jnp.asarray(lengths, jnp.int32))

    lengths = jnp.where(number % 4 == 0, named(heavy_load, number // 4), named(ordinary, number - number // 4 - 1))
    mixed = jax.random.permutation(jax.random.fold_in(own, 3), amount)
    source_of, receiver = mixed[0:amount // 2 * 2:2], mixed[1:amount // 2 * 2:2]
    room = jnp.minimum(lengths[source_of] - 1, reach - lengths[receiver]) // 2
    room = jnp.where((source_of == sequence[0]) | (receiver == sequence[0]) | (lengths[receiver] == 0), 0, jnp.maximum(room, 0))
    passed = jax.random.randint(jax.random.fold_in(own, 4), (amount // 2,), 0, 1 << 20) % (room + 1)
    lengths = lengths.at[source_of].add(-passed).at[receiver].add(passed)
    labels = jnp.searchsorted(jnp.cumsum(lengths), jnp.arange(rows * top), side="right").astype(jnp.int32)
    grid = labels.reshape(top, rows).T
    grid = grid[jax.random.permutation(jax.random.fold_in(own, 1), rows)]
    turn = jax.random.randint(jax.random.fold_in(own, 2), (rows, 1), 0, top)
    return jnp.take_along_axis(grid, (jnp.arange(top)[None, :] + turn) % top, axis=1)


def shares(number_of, total, reach, skew, full):
    loads = [(1 << 20) // math.isqrt(standing ** skew) + 1 for standing in range(1, number_of + 1)]
    largest = reach if full else min(reach, max(-(-total // number_of), total * loads[0] // sum(loads)))
    least = 1 if total - largest >= number_of - 1 else 0
    holding, rest = [largest] + [least] * (number_of - 1), total - largest - least * (number_of - 1)
    while rest > 0:
        movable = [i for i in range(1, number_of) if holding[i] < largest] or [i for i in range(1, number_of) if holding[i] < reach]
        whole, left = sum([loads[i] for i in movable]), rest
        for i in movable:
            addition = min(reach - holding[i], max(1, left * loads[i] // whole), rest)
            holding[i] = holding[i] + addition
            rest = rest - addition
    return np.array(holding)


def scatter_about(rng, dims, spread, limit, shards=(), kind=jnp.bfloat16):
    entries = spread * jax.random.normal(rng, dims, jnp.float32)
    if shards:
        entries = entries * steps_of(rng, dims, shards, -0.22, 0.18)
    return jnp.clip(entries, -limit, limit).astype(kind)


def setup_inputs(seed: int = 0) -> dict:
    keys = jax.random.split(jax.random.key(seed), 7)
    tokens = scatter_about(keys[0], (TOKENS, D), 1.0, 6.0, ((0, 128),))
    routes_keys = jax.random.split(jax.random.fold_in(keys[1], 1), TOKENS // TOK_DEV)
    routes_turns = jax.random.permutation(jax.random.fold_in(keys[1], 3), TOKENS // TOK_DEV)
    routes = jax.vmap(lambda own, number: routed_block(jax.random.fold_in(keys[1], 2), own, number, TOK_DEV, EXPERTS, TOP, CAP, 2))(routes_keys, routes_turns).reshape((TOKENS, TOP))
    router_weight = scatter_about(keys[2], (D, EXPERTS), D ** -0.5, 0.09375)
    gate_weight = scatter_about(keys[3], (EXPERTS, D, FF), D ** -0.5, 0.09375, ((0, 8), (2, 16)))
    up_weight = scatter_about(keys[4], (EXPERTS, D, FF), D ** -0.5, 0.09375, ((0, 8), (2, 16)))
    down_weight = scatter_about(keys[5], (EXPERTS, FF, D), FF ** -0.5, 0.046875, ((0, 8), (1, 16)))
    return dict(tokens=tokens, routes=routes, router_weight=router_weight, gate_weight=gate_weight, up_weight=up_weight, down_weight=down_weight)


def expert_rows(operands):
    buffer_rows, w_gate, w_up, w_down = operands
    arrived = buffer_rows.reshape(-1, D)
    gate_blocks = w_gate.reshape(D, N_SECTION, FF_DEV).transpose(1, 0, 2)
    up_blocks = w_up.reshape(D, N_SECTION, FF_DEV).transpose(1, 0, 2)
    down_blocks = w_down.reshape(N_SECTION, FF_DEV, D)

    def one_block(running, pieces):
        gate_piece, up_piece, down_piece = pieces
        gate_act = jnp.dot(arrived, gate_piece, preferred_element_type=jnp.float32)
        up_act = jnp.dot(arrived, up_piece, preferred_element_type=jnp.float32)
        hidden = (jax.nn.silu(gate_act) * up_act).astype(jnp.bfloat16)
        partial_sum = jnp.dot(hidden, down_piece, preferred_element_type=jnp.float32).astype(jnp.bfloat16)
        partial_sum = lax.optimization_barrier(partial_sum)
        return running + partial_sum.astype(jnp.float32), None

    start_sum = jnp.zeros((arrived.shape[0], D), jnp.float32)
    summed, unused = lax.scan(one_block, start_sum, (gate_blocks, up_blocks, down_blocks))
    return summed.astype(jnp.bfloat16).reshape(buffer_rows.shape)


def reference(tokens, routes, router_weight, gate_weight, up_weight, down_weight):
    logits = jnp.dot(tokens, router_weight, preferred_element_type=jnp.float32)
    chosen = jnp.take_along_axis(logits, routes, axis=1)
    first_gate = jax.nn.sigmoid(chosen[:, 0] - chosen[:, 1])
    gate_pair = jnp.stack([first_gate, 1.0 - first_gate], axis=1)
    onehot = (routes[:, :, None] == jnp.arange(EXPERTS, dtype=jnp.int32)[None, None, :]).astype(jnp.int32)
    block_count = TOKENS // TOK_DEV
    flat_hot = onehot.reshape(block_count, TOK_DEV * TOP, EXPERTS)
    earlier = jnp.cumsum(flat_hot, axis=1) - flat_hot
    slot_index = jnp.sum(earlier * flat_hot, axis=2).reshape(TOKENS, TOP).astype(jnp.int32)
    block_id = (jnp.arange(TOKENS, dtype=jnp.int32) // TOK_DEV).astype(jnp.int32)
    block_pair = jnp.broadcast_to(block_id[:, None], (TOKENS, TOP))
    values = jnp.broadcast_to(tokens[:, None, :], (TOKENS, TOP, D))
    buffer = jnp.zeros((EXPERTS, block_count, CAP, D), jnp.bfloat16)
    buffer = buffer.at[routes, block_pair, slot_index].set(values)
    expert_out = lax.map(expert_rows, (buffer, gate_weight, up_weight, down_weight))
    returned = expert_out[routes, block_pair, slot_index].astype(jnp.float32)
    mixed = jnp.sum(gate_pair[:, :, None] * returned, axis=1)
    return mixed.astype(jnp.bfloat16)
```

```python
import jax
import jax.numpy as jnp
from jax import lax
from jax.sharding import PartitionSpec as P


def shards(tokens, routes, router_weight, gate_weight, up_weight, down_weight):
    tok_rows = tokens.shape[0]
    width_model = tokens.shape[1]
    experts = router_weight.shape[1]
    capacity = tok_rows // 2
    buffer_rows = experts * capacity
    logits = jnp.dot(tokens, router_weight, preferred_element_type=jnp.float32)
    chosen = jnp.take_along_axis(logits, routes, axis=1)
    first_gate = jax.nn.sigmoid(chosen[:, 0] - chosen[:, 1])
    gate_pair = jnp.stack([first_gate, 1.0 - first_gate], axis=1)
    onehot = (routes[:, :, None] == jnp.arange(experts, dtype=jnp.int32)[None, None, :]).astype(
        jnp.int32
    )
    flat_hot = onehot.reshape(tok_rows * 2, experts)
    earlier = jnp.cumsum(flat_hot, axis=0) - flat_hot
    slot_index = jnp.sum(earlier * flat_hot, axis=1).reshape(tok_rows, 2)
    target = routes * capacity + slot_index
    placing = (
        target[:, :, None] == jnp.arange(buffer_rows, dtype=jnp.int32)[None, None, :]
    ).astype(jnp.float32)
    dispatch = jnp.sum(placing, axis=1).astype(jnp.bfloat16)
    outgoing = jnp.dot(dispatch.T, tokens, preferred_element_type=jnp.float32).astype(jnp.bfloat16)
    outgoing = outgoing.reshape(experts, capacity, width_model)
    received = lax.all_to_all(outgoing, "expert", split_axis=0, concat_axis=0, tiled=True)
    arrived = received.reshape(-1, width_model)
    rows = lax.all_gather(arrived, "section", axis=0, tiled=True)
    gate_act = jnp.dot(rows, gate_weight[0], preferred_element_type=jnp.float32)
    up_act = jnp.dot(rows, up_weight[0], preferred_element_type=jnp.float32)
    hidden = (jax.nn.silu(gate_act) * up_act).astype(jnp.bfloat16)
    partial_sum = jnp.dot(hidden, down_weight[0], preferred_element_type=jnp.float32).astype(jnp.bfloat16)
    summed = lax.psum_scatter(partial_sum, "section", scatter_dimension=0, tiled=True)
    expert_out = summed.reshape(experts, capacity, width_model)
    returned = lax.all_to_all(expert_out, "expert", split_axis=0, concat_axis=0, tiled=True)
    combine = jnp.sum(gate_pair[:, :, None] * placing, axis=1)
    mixed = jnp.dot(
        combine,
        returned.reshape(buffer_rows, width_model).astype(jnp.float32),
        precision=lax.Precision.HIGHEST,
    )
    return mixed.astype(jnp.bfloat16)


def solution(mesh):
    in_specs = (
        P(("section", "expert"), None),
        P(("section", "expert"), None),
        P(),
        P("expert", None, "section"),
        P("expert", None, "section"),
        P("expert", "section", None),
    )
    out_specs = P(("section", "expert"), None)
    return jax.shard_map(shards, mesh=mesh, in_specs=in_specs, out_specs=out_specs, check_vma=False)
```

```python
import jax
import jax.numpy as jnp
from jax import lax
from jax.experimental import pallas as pl
from jax.experimental.pallas import tpu as pltpu
from jax.sharding import PartitionSpec as P

MESH = pl.DeviceIdType.MESH
F32, BF16 = jnp.float32, jnp.bfloat16
SIDE = 4
COLOURS = ((0, 1408), (1408, 1408), (2816, 1280))
LANES = 128
VMEM_BYTES = 64 * 1024 * 1024 - 65536


def column_half(start, size, half):
    first = (size // LANES + 1) // 2 * LANES
    return (start, first) if half == 0 else (start + first, size - first)


def spread_dims(colour, phase):
    return sorted((colour + j) % 3 for j in range(phase))


def kernel(x_ref, routes_ref, router_ref, wg_ref, wu_ref, wd_ref, out_ref,
           wgu, wd, rows, meta, xs, staging, acts, hidden, back,
           ra2, rb2, ra1, rb1, ra0, rb0,
           w_sem, ag_send, ag_recv, meta_send, meta_recv, in_send, in_recv, back_send, back_recv,
           rs_send, rs_recv):
    section, expert = lax.axis_index("section"), lax.axis_index("expert")
    core = lax.rem(expert, 2)
    pos = [lax.div(section, SIDE), lax.div(expert, 2), lax.rem(section, SIDE)]
    width = x_ref.shape[1]
    ff = wg_ref.shape[1]
    other_expert = pos[1] * 2 + 1 - core
    twin = (section, other_expert)

    def step(dim, off):
        return lax.rem(pos[dim] + off + SIDE, SIDE)

    def near(dim, off):
        p = list(pos)
        p[dim] = step(dim, off)
        return (p[0] * SIDE + p[2], p[1] * 2 + core)

    loads = [
        pltpu.make_async_copy(wg_ref, wgu.at[:, pl.ds(0, ff)], w_sem.at[0]),
        pltpu.make_async_copy(wu_ref, wgu.at[:, pl.ds(ff, ff)], w_sem.at[1]),
        pltpu.make_async_copy(wd_ref, wd, w_sem.at[2]),
    ]
    for load in loads:
        load.start()

    barrier = pltpu.get_barrier_semaphore()
    greeted = [near(d, o) for d in range(3) for o in (1, -1)] + [twin]
    for device in greeted:
        pl.semaphore_signal(barrier, inc=1, device_id=device, device_id_type=MESH)

    rows[pos[0], pos[1], pos[2]] = x_ref[...]

    tok = x_ref.shape[0]
    logits = lax.dot_general(x_ref[...], router_ref[...], (((1,), (1,)), ((), ())),
                             preferred_element_type=F32)
    first, second = routes_ref[:, 0:1], routes_ref[:, 1:2]
    narrow = lax.broadcasted_iota(jnp.int32, logits.shape, 1)
    gap = (jnp.sum(jnp.where(narrow == first, logits, 0.0), axis=1, keepdims=True)
           - jnp.sum(jnp.where(narrow == second, logits, 0.0), axis=1, keepdims=True))
    gate0 = jax.nn.sigmoid(gap)
    gate1 = 1.0 - gate0
    lane = lax.broadcasted_iota(jnp.int32, (tok, LANES), 1)
    named = jnp.where(lane == first, 1.0, 0.0) + jnp.where(lane == second, 1.0, 0.0)
    below = jnp.where(lax.broadcasted_iota(jnp.int32, (tok, tok), 0)
                      > lax.broadcasted_iota(jnp.int32, (tok, tok), 1), 1.0, 0.0)
    earlier = jnp.dot(below.astype(BF16), named.astype(BF16), preferred_element_type=F32)
    facts = (named * (earlier + 1.0) + jnp.where(lane == first + 8, gate0, 0.0)
             + jnp.where(lane == second + 8, gate1, 0.0))
    meta[pos[0], pos[1], pos[2]] = facts.astype(BF16)

    pl.semaphore_wait(barrier, len(greeted))

    def send(src, dst, sends, recvs, n, device):
        copy = pltpu.make_async_remote_copy(src_ref=src, dst_ref=dst, send_sem=sends.at[n], recv_sem=recvs.at[n],
                                            device_id=device, device_id_type=MESH)
        copy.start()
        return copy

    def piece(ref, colour, phase, at, half):
        start, size = COLOURS[colour]
        dims = spread_dims(colour, phase)
        index = list(pos)
        index[(colour + phase) % 3] = at
        for n, d in enumerate(dims):
            index[d] = pl.ds(0, SIDE)
            if n == 0 and half is not None:
                index[d] = pl.ds(2 * half, 2)
        if phase == 0 and half is not None:
            start, size = column_half(start, size, half)
        return ref.at[index[0], index[1], index[2], :, pl.ds(start, size)]

    pending = []
    for phase in range(3):
        meta_dim = phase
        mi = list(pos)
        for d in range(phase):
            mi[d] = pl.ds(0, SIDE)

        def meta_piece(at):
            index = list(mi)
            index[meta_dim] = at
            return meta.at[index[0], index[1], index[2]]

        mine = meta_piece(pos[meta_dim])
        m_right = send(mine, mine, meta_send, meta_recv, 3 * phase, near(meta_dim, 1))
        m_left = send(mine, mine, meta_send, meta_recv, 3 * phase + 1, near(meta_dim, -1))
        firsts = []
        for colour in range(3):
            dim = (colour + phase) % 3
            base = (phase * 3 + colour) * 6
            got = {}
            for n, (off, half) in enumerate(((1, 0), (-1, 1), (1, 1), (-1, 0))):
                view = piece(rows, colour, phase, pos[dim], half)
                got[off, half] = send(view, view, ag_send, ag_recv, base + n, near(dim, off))
            firsts.append(got)
        m_right.wait_recv()
        view = meta_piece(step(meta_dim, -1))
        m_far = send(view, view, meta_send, meta_recv, 3 * phase + 2, near(meta_dim, 1))
        relays = []
        for colour in range(3):
            dim = (colour + phase) % 3
            base = (phase * 3 + colour) * 6
            for n, (off, half) in enumerate(((1, 0), (-1, 1))):
                firsts[colour][off, half].wait_recv()
                view = piece(rows, colour, phase, step(dim, -off), half)
                relays.append(send(view, view, ag_send, ag_recv, base + 4 + n, near(dim, off)))
        m_left.wait_recv()
        m_far.wait_recv()
        for colour in range(3):
            firsts[colour][1, 1].wait_recv()
            firsts[colour][-1, 0].wait_recv()
        for copy in relays:
            copy.wait_recv()
        pending += [m_right, m_left, m_far] + relays + [c for got in firsts for c in got.values()]
    for copy in pending:
        copy.wait_send()

    groups = 8
    span = 64
    wide = lax.broadcasted_iota(jnp.int32, (LANES, LANES), 1)
    tall = lax.broadcasted_iota(jnp.int32, (LANES, LANES), 0)
    block_of = (lax.div(tall, tok) * 8).astype(F32)[:, 0:1]
    wide_f = wide.astype(F32)

    def placing(g, weighted):
        facts = meta[lax.div(g, 2), pl.ds(lax.rem(g, 2) * 2, 2)].reshape(LANES, LANES).astype(F32)
        total = jnp.zeros((LANES, LANES), F32)
        for which, base in ((expert, 0.0), (other_expert, float(span))):
            slot = jnp.sum(jnp.where(wide == which, facts, 0.0), axis=1, keepdims=True)
            place = jnp.where(slot > 0.5, block_of + slot + (base - 1.0), -1.0)
            value = 1.0
            if weighted:
                value = jnp.sum(jnp.where(wide == which + 8, facts, 0.0), axis=1, keepdims=True)
            total = total + jnp.where(wide_f == place, value, 0.0)
        return total.astype(BF16)

    chunk = 1024
    half_rows = groups * span

    def pick(g, carry):
        place = placing(g, False)
        for n in range(width // chunk):
            cols = pl.ds(n * chunk, chunk)
            block = rows[lax.div(g, 2), pl.ds(lax.rem(g, 2) * 2, 2), :, :, cols].reshape(LANES, chunk)
            got = lax.dot_general(place, block, (((0,), (0,)), ((), ())),
                                  preferred_element_type=F32).astype(BF16)
            xs[pl.ds(pl.multiple_of(g * span, span), span), cols] = got[:span]
            staging[pl.ds(pl.multiple_of(g * span, span), span), cols] = got[span:]
        return carry

    lax.fori_loop(0, groups, pick, 0)
    over = [send(staging.at[pl.ds(q * 256, 256)], xs.at[pl.ds(half_rows + q * 256, 256)],
                 in_send, in_recv, q, twin) for q in range(2)]

    loads[0].wait()
    loads[1].wait()
    tile = 512
    n_tile = 256

    def up_projection(r):
        def one(n, carry):
            cols = pl.ds(pl.multiple_of(n * n_tile, n_tile), n_tile)
            acts[:, cols] = jnp.dot(xs[pl.ds(r * tile, tile)], wgu[:, cols], preferred_element_type=F32)
            return carry

        lax.fori_loop(0, 2 * ff // n_tile, one, 0)

        def squash(i, carry):
            at = pl.ds(pl.multiple_of(i * 32, 32), 32)
            gate = acts[at, pl.ds(0, ff)]
            value = gate / (1.0 + jnp.exp(-gate)) * acts[at, pl.ds(ff, ff)]
            hidden[pl.ds(pl.multiple_of(r * tile + i * 32, 32), 32)] = value.astype(BF16)
            return carry

        lax.fori_loop(0, tile // 32, squash, 0)

    up_projection(0)
    for copy in over:
        copy.wait()
    up_projection(1)
    loads[2].wait()

    returns = []
    quarter = width // 4
    for q in range(4):
        def theirs(n, carry, q=q):
            cols = pl.ds(pl.multiple_of(q * quarter + n * n_tile, n_tile), n_tile)
            staging[:, cols] = jnp.dot(hidden[pl.ds(half_rows, half_rows)], wd[:, cols],
                                       preferred_element_type=F32).astype(BF16)
            return carry

        lax.fori_loop(0, quarter // n_tile, theirs, 0)
        cols = pl.ds(q * quarter, quarter)
        returns.append(send(staging.at[:, cols], back.at[:, cols], back_send, back_recv, q, twin))

    def mine(n, carry):
        cols = pl.ds(pl.multiple_of(n * n_tile, n_tile), n_tile)
        xs[pl.ds(0, half_rows), cols] = jnp.dot(hidden[pl.ds(0, half_rows)], wd[:, cols],
                                                preferred_element_type=F32).astype(BF16)
        return carry

    lax.fori_loop(0, width // n_tile, mine, 0)
    for copy in returns:
        copy.wait()

    def mix(g, carry):
        place = placing(g, True)
        at = pl.ds(pl.multiple_of(g * span, span), span)
        for n in range(width // chunk):
            cols = pl.ds(n * chunk, chunk)
            both = jnp.concatenate([xs[at, cols], back[at, cols]], axis=0)
            got = jnp.dot(place, both, preferred_element_type=F32).astype(BF16)
            rows[lax.div(g, 2), pl.ds(lax.rem(g, 2) * 2, 2), :, :, cols] = got.reshape(2, SIDE, tok, chunk)
        return carry

    lax.fori_loop(0, groups, mix, 0)

    def landing(ref, colour, phase, way, half):
        start, size = COLOURS[colour]
        if phase == 0:
            if half is not None:
                start, size = column_half(start, size, half)
            return ref.at[way, :, pl.ds(start, size)]
        lead = pl.ds(0, ref.shape[1]) if half is None else pl.ds(2 * half, 2)
        if phase == 1:
            return ref.at[way, lead, :, pl.ds(start, size)]
        return ref.at[way, lead, :, :, pl.ds(start, size)]

    def add_in(colour, phase, at, half, parts):
        start, size = COLOURS[colour]
        dims = spread_dims(colour, phase)
        if phase == 0 and half is not None:
            start, size = column_half(start, size, half)
        cols = pl.ds(start, size)

        def one(i, carry):
            index = list(pos)
            index[(colour + phase) % 3] = at
            if phase == 2:
                lead, low = lax.div(i, SIDE), lax.rem(i, SIDE)
                index[dims[1]] = low
            else:
                lead, low = i, None
            if phase >= 1:
                index[dims[0]] = lead if half is None else lead + 2 * half
            total = rows[index[0], index[1], index[2], :, cols].astype(F32)
            for ref, way in parts:
                if phase == 0:
                    total = total + ref[way, :, cols].astype(F32)
                elif phase == 1:
                    total = total + ref[way, lead, :, cols].astype(F32)
                else:
                    total = total + ref[way, lead, low, :, cols].astype(F32)
            rows[index[0], index[1], index[2], :, cols] = total.astype(BF16)
            return carry

        count = (SIDE if half is None else 2) if phase >= 1 else 1
        count = count * SIDE if phase == 2 else count
        lax.fori_loop(0, count, one, 0)

    pending = []
    for phase, ra, rb in ((2, ra2, rb2), (1, ra1, rb1), (0, ra0, rb0)):
        fars, seconds = [], []
        for colour in range(3):
            dim = (colour + phase) % 3
            base = (phase * 3 + colour) * 6
            far, second = {}, {}
            for n, (off, half, way) in enumerate(((1, 0, 0), (-1, 1, 1))):
                far[off] = send(piece(rows, colour, phase, step(dim, 2), half),
                                landing(ra, colour, phase, way, half if phase == 0 else None),
                                rs_send, rs_recv, base + n, near(dim, off))
            for n, (off, half, way) in enumerate(((1, 1, 0), (-1, 0, 1))):
                second[off, half] = send(piece(rows, colour, phase, step(dim, off), half),
                                         landing(rb, colour, phase, way, half),
                                         rs_send, rs_recv, base + 2 + n, near(dim, off))
            fars.append(far)
            seconds.append(second)
        for colour in range(3):
            dim = (colour + phase) % 3
            base = (phase * 3 + colour) * 6
            for n, (off, half, way) in enumerate(((1, 0, 0), (-1, 1, 1))):
                fars[colour][off].wait_recv()
                add_in(colour, phase, step(dim, off), half, [(ra, way)])
                seconds[colour][off, half] = send(piece(rows, colour, phase, step(dim, off), half),
                                                  landing(rb, colour, phase, way, half),
                                                  rs_send, rs_recv, base + 4 + n, near(dim, off))
        for colour in range(3):
            dim = (colour + phase) % 3
            for copy in seconds[colour].values():
                copy.wait_recv()
            add_in(colour, phase, pos[dim], None, [(rb, 0), (rb, 1)])
        pending += [c for far in fars for c in far.values()] + [c for sec in seconds for c in sec.values()]
    for copy in pending:
        copy.wait_send()
    out_ref[...] = rows[pos[0], pos[1], pos[2]]


def shards(tokens, routes, router_weight, gate_weight, up_weight, down_weight):
    tok, width = tokens.shape
    ff = gate_weight.shape[2]
    blocks = (SIDE, SIDE, SIDE)
    vmem = pl.BlockSpec(memory_space=pltpu.VMEM)
    anywhere = pl.BlockSpec(memory_space=pl.ANY)
    dma = pltpu.SemaphoreType.DMA
    return pl.pallas_call(
        kernel,
        out_shape=jax.ShapeDtypeStruct((tok, width), BF16),
        in_specs=[vmem, vmem, vmem, anywhere, anywhere, anywhere],
        out_specs=vmem,
        scratch_shapes=[
            pltpu.VMEM((width, 2 * ff), BF16),
            pltpu.VMEM((ff, width), BF16),
            pltpu.VMEM(blocks + (tok, width), BF16),
            pltpu.VMEM(blocks + (tok, LANES), BF16),
            pltpu.VMEM((1024, width), BF16),
            pltpu.VMEM((512, width), BF16),
            pltpu.VMEM((512, 2 * ff), F32),
            pltpu.VMEM((1024, ff), BF16),
            pltpu.VMEM((512, width), BF16),
            pltpu.VMEM((2, 2, SIDE, tok, width), BF16),
            pltpu.VMEM((2, SIDE, SIDE, tok, width), BF16),
            pltpu.VMEM((2, 2, tok, width), BF16),
            pltpu.VMEM((2, SIDE, tok, width), BF16),
            pltpu.VMEM((2, tok, width), BF16),
            pltpu.VMEM((2, tok, width), BF16),
            dma((3,)),
            dma((54,)), dma((54,)),
            dma((9,)), dma((9,)),
            dma((2,)), dma((2,)),
            dma((4,)), dma((4,)),
            dma((54,)), dma((54,)),
        ],
        compiler_params=pltpu.CompilerParams(
            collective_id=0, has_side_effects=True, vmem_limit_bytes=VMEM_BYTES
        ),
        cost_estimate=pl.CostEstimate(flops=2 * 3 * 1024 * width * ff, bytes_accessed=6 * ff * width,
                                      transcendentals=1024 * ff),
    )(tokens, routes, router_weight.T, gate_weight[0], up_weight[0], down_weight[0])


def solution(mesh):
    in_specs = (
        P(("section", "expert"), None),
        P(("section", "expert"), None),
        P(),
        P("expert", None, "section"),
        P("expert", None, "section"),
        P("expert", "section", None),
    )
    out_specs = P(("section", "expert"), None)
    return jax.shard_map(shards, mesh=mesh, in_specs=in_specs, out_specs=out_specs, check_vma=False)
```

```python
import jax
import jax.numpy as jnp
from jax import lax
from jax.experimental import pallas as pl
from jax.experimental.pallas import tpu as pltpu
from jax.sharding import PartitionSpec as P

MESH = pl.DeviceIdType.MESH
F32, BF16 = jnp.float32, jnp.bfloat16
SIDE = 4
WAVES = 2
COLOURS = (((0, 768), (768, 640), (1408, 640)), ((0, 640), (640, 768), (1408, 640)))
LANES = 128
VMEM_BYTES = 64 * 1024 * 1024 - 65536
OFFSETS = (1, -1, 2)


def spread_dims(colour, phase):
    return sorted((colour + j) % 3 for j in range(phase))


def kernel(x_ref, routes_ref, router_ref, wg_ref, wu_ref, wd_ref, out_ref,
           wgu, wd, rows, meta, xs, staging, outgoing, acts, hidden, back, final,
           ra2, rb2, r1, r0,
           w_sem, ag_send, ag_recv, meta_send, meta_recv, swap_send, swap_recv, in_send, in_recv,
           back_send, back_recv, rs_send, rs_recv):
    section, expert = lax.axis_index("section"), lax.axis_index("expert")
    core = lax.rem(expert, 2)
    pos = [lax.div(section, SIDE), lax.div(expert, 2), lax.rem(section, SIDE)]
    tok, width = x_ref.shape
    half_width = width // 2
    ff = wg_ref.shape[1]
    other_expert = pos[1] * 2 + 1 - core
    twin = (section, other_expert)
    my_start = pl.multiple_of(core * half_width, half_width)
    twin_start = pl.multiple_of((1 - core) * half_width, half_width)

    def step(dim, off):
        return lax.rem(pos[dim] + off + SIDE, SIDE)

    def near(dim, off):
        p = list(pos)
        p[dim] = step(dim, off)
        return (p[0] * SIDE + p[2], p[1] * 2 + core)

    loads = [
        pltpu.make_async_copy(wg_ref, wgu.at[:, pl.ds(0, ff)], w_sem.at[0]),
        pltpu.make_async_copy(wu_ref, wgu.at[:, pl.ds(ff, ff)], w_sem.at[1]),
        pltpu.make_async_copy(wd_ref, wd, w_sem.at[2]),
    ]

    barrier = pltpu.get_barrier_semaphore()
    greeted = [near(d, o) for d in range(3) for o in OFFSETS] + [twin]
    for device in greeted:
        pl.semaphore_signal(barrier, inc=1, device_id=device, device_id_type=MESH)
    for load in loads:
        load.start()

    rows[core, pos[0], pos[1], pos[2]] = x_ref[:, pl.ds(my_start, half_width)]

    def send(src, dst, sends, recvs, n, device):
        copy = pltpu.make_async_remote_copy(src_ref=src, dst_ref=dst, send_sem=sends.at[n], recv_sem=recvs.at[n],
                                            device_id=device, device_id_type=MESH)
        copy.start()
        return copy

    pl.semaphore_wait(barrier, len(greeted))
    swap = send(x_ref.at[:, pl.ds(twin_start, half_width)], rows.at[core, pos[0], pos[1], pos[2]],
                swap_send, swap_recv, 0, twin)

    logits = lax.dot_general(x_ref[...], router_ref[...], (((1,), (1,)), ((), ())),
                             preferred_element_type=F32)
    first, second = routes_ref[:, 0:1], routes_ref[:, 1:2]
    narrow = lax.broadcasted_iota(jnp.int32, logits.shape, 1)
    gap = (jnp.sum(jnp.where(narrow == first, logits, 0.0), axis=1, keepdims=True)
           - jnp.sum(jnp.where(narrow == second, logits, 0.0), axis=1, keepdims=True))
    gate0 = jax.nn.sigmoid(gap)
    gate1 = 1.0 - gate0
    lane = lax.broadcasted_iota(jnp.int32, (tok, LANES), 1)
    named = jnp.where(lane == first, 1.0, 0.0) + jnp.where(lane == second, 1.0, 0.0)
    below = jnp.where(lax.broadcasted_iota(jnp.int32, (tok, tok), 0)
                      > lax.broadcasted_iota(jnp.int32, (tok, tok), 1), 1.0, 0.0)
    earlier = jnp.dot(below.astype(BF16), named.astype(BF16), preferred_element_type=F32)
    facts = (named * (earlier + 1.0) + jnp.where(lane == first + 8, gate0, 0.0)
             + jnp.where(lane == second + 8, gate1, 0.0))
    meta[core, pos[0], pos[1], pos[2]] = facts.astype(BF16)

    def piece(wave, colour, phase, at, half):
        start, size = COLOURS[wave][colour]
        index = list(pos)
        index[(colour + phase) % 3] = at
        for n, d in enumerate(spread_dims(colour, phase)):
            index[d] = pl.ds(0, SIDE) if n or half is None else pl.ds(2 * half, 2)
        return rows.at[wave, index[0], index[1], index[2], :, pl.ds(start, size)]

    class Gather:
        def __init__(self, wave):
            self.wave, self.all, self.last = wave, [], []

        def number(self, phase, colour, n):
            return self.wave * 36 + (colour * 3 + n if phase < 2 else 18 + colour * 6 + n) + 9 * (phase == 1)

        def send(self, phase, colour, n, view, off):
            copy = send(view, view, ag_send, ag_recv, self.number(phase, colour, n), near((colour + phase) % 3, off))
            self.all.append(copy)
            return copy

        def arrive(self):
            for copy in self.last:
                copy.wait_recv()

        def direct(self, phase):
            self.arrive()
            self.last = []
            for n, off in enumerate(OFFSETS):
                for colour in range(3):
                    view = piece(self.wave, colour, phase, pos[(colour + phase) % 3], None)
                    self.last.append(self.send(phase, colour, n, view, off))

        def planes(self):
            self.arrive()
            self.last, self.relayed = [], []
            for n, (off, half) in enumerate(((1, 0), (-1, 1), (1, 1), (-1, 0))):
                for colour in range(3):
                    view = piece(self.wave, colour, 2, pos[(colour + 2) % 3], half)
                    copy = self.send(2, colour, n, view, off)
                    (self.relayed if n < 2 else self.last).append((colour, off, half, copy) if n < 2 else copy)

        def relay(self):
            for n, (colour, off, half, copy) in enumerate(self.relayed):
                copy.wait_recv()
                view = piece(self.wave, colour, 2, step((colour + 2) % 3, -off), half)
                self.last.append(self.send(2, colour, 4 + n // 3, view, off))

        def drain(self):
            for copy in self.all:
                copy.wait_send()

    meta_copies = []

    def meta_step(phase):
        for copy in meta_copies[-3:]:
            copy.wait_recv()
        if phase == 3:
            return send(meta.at[core], meta.at[core], meta_send, meta_recv, 9, twin)
        index = [pl.ds(0, SIDE) if d < phase else pos[d] for d in range(3)]
        view = meta.at[core, index[0], index[1], index[2]]
        for n, off in enumerate(OFFSETS):
            meta_copies.append(send(view, view, meta_send, meta_recv, 3 * phase + n, near(phase, off)))

    swap.wait_recv()
    g0, g1 = Gather(0), Gather(1)
    g0.direct(0)
    meta_step(0)
    g1.direct(0)
    g0.direct(1)
    meta_step(1)
    g0.planes()
    meta_step(2)
    g0.relay()
    g1.direct(1)
    meta_swap = meta_step(3)
    g0.arrive()
    meta_swap.wait_recv()

    groups = 8
    span = 64
    wide = lax.broadcasted_iota(jnp.int32, (LANES, LANES), 1)
    tall = lax.broadcasted_iota(jnp.int32, (LANES, LANES), 0)
    block_of = (lax.div(tall, tok) * 8).astype(F32)[:, 0:1]
    wide_f = wide.astype(F32)

    def placing(wave, g, weighted):
        facts = meta[wave, lax.div(g, 2), pl.ds(lax.rem(g, 2) * 2, 2)].reshape(LANES, LANES).astype(F32)
        total = jnp.zeros((LANES, LANES), F32)
        for which, base in ((expert, 0.0), (other_expert, float(span))):
            slot = jnp.sum(jnp.where(wide == which, facts, 0.0), axis=1, keepdims=True)
            place = jnp.where(slot > 0.5, block_of + slot + (base - 1.0), -1.0)
            value = 1.0
            if weighted:
                value = jnp.sum(jnp.where(wide == which + 8, facts, 0.0), axis=1, keepdims=True)
            total = total + jnp.where(wide_f == place, value, 0.0)
        return total.astype(BF16)

    chunk = 1024
    n_tile = 256
    tile = 256
    slots = groups * span

    def pick(wave, part):
        def one(g, carry):
            place = placing(wave, g, False)
            at = pl.ds(pl.multiple_of(g * span, span), span)
            for n in range(half_width // chunk):
                block = rows[wave, lax.div(g, 2), pl.ds(lax.rem(g, 2) * 2, 2), :, :, pl.ds(n * chunk, chunk)]
                got = lax.dot_general(place, block.reshape(LANES, chunk), (((0,), (0,)), ((), ())),
                                      preferred_element_type=F32).astype(BF16)
                xs[wave, at, pl.ds(pl.multiple_of(my_start + n * chunk, chunk), chunk)] = got[:span]
                staging[at, pl.ds(n * chunk, chunk)] = got[span:]
            return carry

        lax.fori_loop(part * 4, part * 4 + 4, one, 0)
        at = pl.ds(part * 256, 256)
        return send(staging.at[at], xs.at[wave, at, pl.ds(my_start, half_width)],
                    in_send, in_recv, wave * 2 + part, twin)

    def up_projection(wave, r):
        def one(n, carry):
            cols = pl.ds(pl.multiple_of(n * n_tile, n_tile), n_tile)
            acts[:, cols] = jnp.dot(xs[wave], wgu[:, cols], preferred_element_type=F32)
            return carry

        lax.fori_loop(0, 2 * ff // n_tile, one, 0)

        def squash(i, carry):
            at = pl.ds(pl.multiple_of(i * 32, 32), 32)
            gate = acts[at, pl.ds(0, ff)]
            hidden[at] = (gate / (1.0 + jnp.exp(-gate)) * acts[at, pl.ds(ff, ff)]).astype(BF16)
            return carry

        lax.fori_loop(0, slots // 32, squash, 0)

    def down_twin(wave, part):
        quarter = half_width // 2

        def one(n, carry):
            at = part * quarter + n * n_tile
            outgoing[:, pl.ds(pl.multiple_of(at, n_tile), n_tile)] = jnp.dot(
                hidden[...], wd[:, pl.ds(pl.multiple_of(twin_start + at, n_tile), n_tile)],
                preferred_element_type=F32).astype(BF16)
            return carry

        lax.fori_loop(0, quarter // n_tile, one, 0)
        cols = pl.ds(part * quarter, quarter)
        return send(outgoing.at[:, cols], back.at[wave, :, cols], back_send, back_recv, wave * 2 + part, twin)

    def down_mine(wave):
        def one(n, carry):
            at = n * n_tile
            xs[wave, :, pl.ds(pl.multiple_of(at, n_tile), n_tile)] = jnp.dot(
                hidden[...], wd[:, pl.ds(pl.multiple_of(my_start + at, n_tile), n_tile)],
                preferred_element_type=F32).astype(BF16)
            return carry

        lax.fori_loop(0, half_width // n_tile, one, 0)

    def mix(wave):
        def one(g, carry):
            place = placing(wave, g, True)
            at = pl.ds(pl.multiple_of(g * span, span), span)
            for n in range(half_width // chunk):
                cols = pl.ds(n * chunk, chunk)
                both = jnp.concatenate([xs[wave, at, cols], back[wave, at, cols]], axis=0)
                got = jnp.dot(place, both, preferred_element_type=F32).astype(BF16)
                rows[wave, lax.div(g, 2), pl.ds(lax.rem(g, 2) * 2, 2), :, :, cols] = got.reshape(2, SIDE, tok, chunk)
            return carry

        lax.fori_loop(0, groups, one, 0)

    class Scatter:
        def __init__(self, wave):
            self.wave, self.all = wave, []

        def send(self, phase, colour, n, view, landing, off):
            number = self.wave * 36 + (18 + colour * 6 + n if phase == 2 else 9 * phase + colour * 3 + n)
            copy = send(view, landing, rs_send, rs_recv, number, near((colour + phase) % 3, off))
            self.all.append(copy)
            return copy

        def land(self, ref, colour, phase, way, half):
            cols = pl.ds(*COLOURS[self.wave][colour])
            if phase == 0:
                return ref.at[self.wave, way, :, cols]
            lead = pl.ds(0, ref.shape[2]) if half is None else pl.ds(2 * half, 2)
            if phase == 1:
                return ref.at[self.wave, way, lead, :, cols]
            return ref.at[self.wave, way, lead, :, :, cols]

        def add(self, colour, phase, at, half, ref, ways):
            cols = pl.ds(*COLOURS[self.wave][colour])
            dims = spread_dims(colour, phase)

            def one(i, carry):
                index = list(pos)
                index[(colour + phase) % 3] = at
                lead, low = (lax.div(i, SIDE), lax.rem(i, SIDE)) if phase == 2 else (i, None)
                if phase == 2:
                    index[dims[1]] = low
                if phase >= 1:
                    index[dims[0]] = lead if half is None else lead + 2 * half
                here = (self.wave, index[0], index[1], index[2], slice(None), cols)
                total = rows[here].astype(F32)
                for way in ways:
                    where = {0: (way,), 1: (way, lead), 2: (way, lead, low)}[phase]
                    total = total + ref[(self.wave,) + where + (slice(None), cols)].astype(F32)
                rows[here] = total.astype(BF16)
                return carry

            count = (SIDE if half is None else 2) if phase >= 1 else 1
            lax.fori_loop(0, count * SIDE if phase == 2 else count, one, 0)

        def planes(self):
            self.fars, self.seconds = [], []
            for n, (off, half) in enumerate(((1, 0), (-1, 1))):
                for colour in range(3):
                    at = step((colour + 2) % 3, 2)
                    self.fars.append((colour, off, half, n, self.send(
                        2, colour, n, piece(self.wave, colour, 2, at, half),
                        self.land(ra2, colour, 2, n, None), off)))
            for n, (off, half) in enumerate(((1, 1), (-1, 0))):
                for colour in range(3):
                    at = step((colour + 2) % 3, off)
                    self.seconds.append(self.send(
                        2, colour, 2 + n, piece(self.wave, colour, 2, at, half),
                        self.land(rb2, colour, 2, n, half), off))

        def relay(self):
            for colour, off, half, n, copy in self.fars:
                copy.wait_recv()
                at = step((colour + 2) % 3, off)
                self.add(colour, 2, at, half, ra2, (n,))
                self.seconds.append(self.send(2, colour, 4 + n, piece(self.wave, colour, 2, at, half),
                                              self.land(rb2, colour, 2, n, half), off))

        def own_plane(self):
            for copy in self.seconds:
                copy.wait_recv()
            for colour in range(3):
                self.add(colour, 2, pos[(colour + 2) % 3], None, rb2, (0, 1))

        def direct(self, phase):
            ref = r1 if phase == 1 else r0
            self.last = []
            for n, off in ((2, 2), (0, 1), (1, -1)):
                for colour in range(3):
                    at = step((colour + phase) % 3, off)
                    self.last.append(self.send(phase, colour, n, piece(self.wave, colour, phase, at, None),
                                               self.land(ref, colour, phase, n, None), off))

        def settle(self, phase):
            ref = r1 if phase == 1 else r0
            for copy in self.last:
                copy.wait_recv()
            for colour in range(3):
                self.add(colour, phase, pos[(colour + phase) % 3], None, ref, (0, 1, 2))

        def drain(self):
            for copy in self.all:
                copy.wait_send()

    picked0 = [pick(0, 0)]
    g1.planes()
    picked0.append(pick(0, 1))
    loads[0].wait()
    loads[1].wait()
    for copy in picked0:
        copy.wait()
    up_projection(0, 0)
    g1.relay()
    loads[2].wait()
    sent0 = [down_twin(0, 0), down_twin(0, 1)]
    down_mine(0)
    g0.drain()
    for copy in sent0:
        copy.wait()
    mix(0)
    s0, s1 = Scatter(0), Scatter(1)
    s0.planes()
    g1.arrive()
    picked1 = [pick(1, 0), pick(1, 1)]
    s0.relay()
    for copy in picked1:
        copy.wait()
    up_projection(1, 0)
    sent1 = [down_twin(1, 0), down_twin(1, 1)]
    s0.own_plane()
    s0.direct(1)
    down_mine(1)
    g1.drain()
    for copy in sent1:
        copy.wait()
    mix(1)
    s1.planes()
    s0.settle(1)
    s0.direct(0)
    s1.relay()
    s0.settle(0)
    s1.own_plane()
    s1.direct(1)
    s1.settle(1)
    s1.direct(0)
    s1.settle(0)
    swap.wait_send()
    ending = send(rows.at[1 - core, pos[0], pos[1], pos[2]], final, swap_send, swap_recv, 1, twin)
    out_ref[:, pl.ds(my_start, half_width)] = rows[core, pos[0], pos[1], pos[2]]
    for copy in meta_copies + [meta_swap]:
        copy.wait_send()
    s0.drain()
    s1.drain()
    ending.wait()
    out_ref[:, pl.ds(twin_start, half_width)] = final[...]


def shards(tokens, routes, router_weight, gate_weight, up_weight, down_weight):
    tok, width = tokens.shape
    half = width // 2
    ff = gate_weight.shape[2]
    cube = (WAVES, SIDE, SIDE, SIDE)
    vmem = pl.BlockSpec(memory_space=pltpu.VMEM)
    anywhere = pl.BlockSpec(memory_space=pl.ANY)
    dma = pltpu.SemaphoreType.DMA
    return pl.pallas_call(
        kernel,
        out_shape=jax.ShapeDtypeStruct((tok, width), BF16),
        in_specs=[vmem, vmem, vmem, anywhere, anywhere, anywhere],
        out_specs=vmem,
        scratch_shapes=[
            pltpu.VMEM((width, 2 * ff), BF16),
            pltpu.VMEM((ff, width), BF16),
            pltpu.VMEM(cube + (tok, half), BF16),
            pltpu.VMEM(cube + (tok, LANES), BF16),
            pltpu.VMEM((WAVES, 512, width), BF16),
            pltpu.VMEM((512, half), BF16),
            pltpu.VMEM((512, half), BF16),
            pltpu.VMEM((512, 2 * ff), F32),
            pltpu.VMEM((512, ff), BF16),
            pltpu.VMEM((WAVES, 512, half), BF16),
            pltpu.VMEM((tok, half), BF16),
            pltpu.VMEM((WAVES, 2, 2, SIDE, tok, half), BF16),
            pltpu.VMEM((WAVES, 2, SIDE, SIDE, tok, half), BF16),
            pltpu.VMEM((WAVES, 3, SIDE, tok, half), BF16),
            pltpu.VMEM((WAVES, 3, tok, half), BF16),
            dma((3,)),
            dma((72,)), dma((72,)),
            dma((10,)), dma((10,)),
            dma((2,)), dma((2,)),
            dma((4,)), dma((4,)),
            dma((4,)), dma((4,)),
            dma((72,)), dma((72,)),
        ],
        compiler_params=pltpu.CompilerParams(
            collective_id=0, has_side_effects=True, vmem_limit_bytes=VMEM_BYTES
        ),
        cost_estimate=pl.CostEstimate(flops=2 * 3 * 1024 * width * ff, bytes_accessed=6 * ff * width,
                                      transcendentals=1024 * ff),
    )(tokens, routes, router_weight.T, gate_weight[0], up_weight[0], down_weight[0])


def solution(mesh):
    in_specs = (
        P(("section", "expert"), None),
        P(("section", "expert"), None),
        P(),
        P("expert", None, "section"),
        P("expert", None, "section"),
        P("expert", "section", None),
    )
    out_specs = P(("section", "expert"), None)
    return jax.shard_map(shards, mesh=mesh, in_specs=in_specs, out_specs=out_specs, check_vma=False)
```

```python
import jax
import jax.numpy as jnp
from jax import lax
from jax.experimental import pallas as pl
from jax.experimental.pallas import tpu as pltpu
from jax.sharding import PartitionSpec as P

MESH = pl.DeviceIdType.MESH
F32, BF16 = jnp.float32, jnp.bfloat16
SIDE = 4
WAVES = 2
FORTH = ((0, 768), (768, 768), (1536, 640))
BACK = ((0, 768), (768, 640), (1408, 640))
LANES = 128
VMEM_BYTES = 64 * 1024 * 1024 - 65536
OFFSETS = (1, -1, 2)


def spread_dims(colour, phase):
    return sorted((colour + j) % 3 for j in range(phase))


def kernel(x_ref, routes_ref, router_ref, wg_ref, wu_ref, wd_ref, out_ref,
           wgu, wd, rows, places, xs, staging, outgoing, acts, hidden, back, final,
           ra2, rb2, r1, r0,
           w_sem, ag_send, ag_recv, swap_send, swap_recv, in_send, in_recv,
           back_send, back_recv, rs_send, rs_recv):
    section, expert = lax.axis_index("section"), lax.axis_index("expert")
    core = lax.rem(expert, 2)
    pos = [lax.div(section, SIDE), lax.div(expert, 2), lax.rem(section, SIDE)]
    tok, width = x_ref.shape
    half_width = width // 2
    ff = wg_ref.shape[1]
    other_expert = pos[1] * 2 + 1 - core
    twin = (section, other_expert)
    my_start = pl.multiple_of(core * half_width, half_width)
    twin_start = pl.multiple_of((1 - core) * half_width, half_width)

    def step(dim, off):
        return lax.rem(pos[dim] + off + SIDE, SIDE)

    def near(dim, off):
        p = list(pos)
        p[dim] = step(dim, off)
        return (p[0] * SIDE + p[2], p[1] * 2 + core)

    loads = [
        pltpu.make_async_copy(wg_ref, wgu.at[:, pl.ds(0, ff)], w_sem.at[0]),
        pltpu.make_async_copy(wu_ref, wgu.at[:, pl.ds(ff, ff)], w_sem.at[1]),
        pltpu.make_async_copy(wd_ref, wd, w_sem.at[2]),
    ]

    barrier = pltpu.get_barrier_semaphore()
    greeted = [near(d, o) for d in range(3) for o in OFFSETS] + [twin]
    for device in greeted:
        pl.semaphore_signal(barrier, inc=1, device_id=device, device_id_type=MESH)
    for load in loads:
        load.start()

    body = pl.ds(0, half_width)
    tail = pl.ds(half_width, LANES)
    rows[core, pos[0], pos[1], pos[2], :, body] = x_ref[:, pl.ds(my_start, half_width)]

    logits = lax.dot_general(x_ref[...], router_ref[...], (((1,), (1,)), ((), ())),
                             preferred_element_type=F32)
    square = (tok, tok)
    down_rows, over_lanes = lax.broadcasted_iota(jnp.int32, square, 0), lax.broadcasted_iota(jnp.int32, square, 1)

    def upright(k):
        spread = jnp.broadcast_to(routes_ref[k:k + 1, :], square)
        return jnp.sum(jnp.where(down_rows == over_lanes, spread, 0), axis=1, keepdims=True)

    first, second = upright(0), upright(1)
    narrow = lax.broadcasted_iota(jnp.int32, logits.shape, 1)
    gap = (jnp.sum(jnp.where(narrow == first, logits, 0.0), axis=1, keepdims=True)
           - jnp.sum(jnp.where(narrow == second, logits, 0.0), axis=1, keepdims=True))
    gate0 = jax.nn.sigmoid(gap)
    gate1 = 1.0 - gate0
    lane = lax.broadcasted_iota(jnp.int32, (tok, LANES), 1)
    named = jnp.where(lane == first, 1.0, 0.0) + jnp.where(lane == second, 1.0, 0.0)
    below = jnp.where(down_rows > over_lanes, 1.0, 0.0)
    earlier = jnp.dot(below.astype(BF16), named.astype(BF16), preferred_element_type=F32)
    facts = (named * (earlier + 1.0) + jnp.where(lane == first + 8, gate0, 0.0)
             + jnp.where(lane == second + 8, gate1, 0.0))
    rows[core, pos[0], pos[1], pos[2], :, tail] = facts.astype(BF16)

    def send(src, dst, sends, recvs, n, device):
        copy = pltpu.make_async_remote_copy(src_ref=src, dst_ref=dst, send_sem=sends.at[n], recv_sem=recvs.at[n],
                                            device_id=device, device_id_type=MESH)
        copy.start()
        return copy

    pl.semaphore_wait(barrier, len(greeted))
    swap = send(x_ref.at[:, pl.ds(twin_start, half_width)], rows.at[core, pos[0], pos[1], pos[2], :, body],
                swap_send, swap_recv, 0, twin)

    own_facts = rows.at[core, pos[0], pos[1], pos[2], :, tail]
    swap_facts = send(own_facts, own_facts, swap_send, swap_recv, 2, twin)

    def piece(wave, colour, phase, at, half, colours):
        start, size = colours[colour]
        index = list(pos)
        index[(colour + phase) % 3] = at
        for n, d in enumerate(spread_dims(colour, phase)):
            index[d] = pl.ds(0, SIDE) if n or half is None else pl.ds(2 * half, 2)
        return rows.at[wave, index[0], index[1], index[2], :, pl.ds(start, size)]

    class Gather:
        def __init__(self, wave):
            self.wave, self.all, self.last = wave, [], []

        def number(self, phase, colour, n):
            return self.wave * 36 + (colour * 3 + n if phase < 2 else 18 + colour * 6 + n) + 9 * (phase == 1)

        def send(self, phase, colour, n, view, off):
            copy = send(view, view, ag_send, ag_recv, self.number(phase, colour, n), near((colour + phase) % 3, off))
            self.all.append(copy)
            return copy

        def arrive(self):
            for copy in self.last:
                copy.wait_recv()

        def direct(self, phase):
            self.arrive()
            self.last = []
            for n, off in enumerate(OFFSETS):
                for colour in range(3):
                    view = piece(self.wave, colour, phase, pos[(colour + phase) % 3], None, FORTH)
                    self.last.append(self.send(phase, colour, n, view, off))

        def planes(self):
            self.arrive()
            self.last, self.relayed = [], []
            for n, (off, half) in enumerate(((1, 0), (-1, 1), (1, 1), (-1, 0))):
                for colour in range(3):
                    view = piece(self.wave, colour, 2, pos[(colour + 2) % 3], half, FORTH)
                    copy = self.send(2, colour, n, view, off)
                    (self.relayed if n < 2 else self.last).append((colour, off, half, copy) if n < 2 else copy)

        def relay(self):
            for n, (colour, off, half, copy) in enumerate(self.relayed):
                copy.wait_recv()
                view = piece(self.wave, colour, 2, step((colour + 2) % 3, -off), half, FORTH)
                self.last.append(self.send(2, colour, 4 + n // 3, view, off))

        def drain(self):
            for copy in self.all:
                copy.wait_send()

    swap.wait_recv()
    swap_facts.wait_recv()
    g0, g1 = Gather(0), Gather(1)
    g0.direct(0)
    g1.direct(0)
    g0.direct(1)
    g1.direct(1)
    g0.planes()
    g0.relay()
    g0.arrive()

    groups = 8
    span = 64
    wide = lax.broadcasted_iota(jnp.int32, (LANES, LANES), 1)
    tall = lax.broadcasted_iota(jnp.int32, (LANES, LANES), 0)
    block_of = (lax.div(tall, tok) * 8).astype(F32)[:, 0:1]
    wide_f = wide.astype(F32)

    def placing(wave, g):
        facts = rows[wave, lax.div(g, 2), pl.ds(lax.rem(g, 2) * 2, 2), :, :, tail].reshape(LANES, LANES).astype(F32)
        plain = jnp.zeros((LANES, LANES), F32)
        weighted = jnp.zeros((LANES, LANES), F32)
        for which, base in ((expert, 0.0), (other_expert, float(span))):
            slot = jnp.sum(jnp.where(wide == which, facts, 0.0), axis=1, keepdims=True)
            gate = jnp.sum(jnp.where(wide == which + 8, facts, 0.0), axis=1, keepdims=True)
            hit = wide_f == jnp.where(slot > 0.5, block_of + slot + (base - 1.0), -1.0)
            plain = jnp.where(hit, 1.0, plain)
            weighted = jnp.where(hit, gate, weighted)
        places[wave, g] = weighted.astype(BF16)
        return plain.astype(BF16)

    chunk = 1024
    n_tile = 256
    tile = 256
    slots = groups * span

    def pick(wave, part):
        def one(g, carry):
            place = placing(wave, g)
            at = pl.ds(pl.multiple_of(g * span, span), span)
            for n in range(half_width // chunk):
                block = rows[wave, lax.div(g, 2), pl.ds(lax.rem(g, 2) * 2, 2), :, :, pl.ds(n * chunk, chunk)]
                got = lax.dot_general(place, block.reshape(LANES, chunk), (((0,), (0,)), ((), ())),
                                      preferred_element_type=F32).astype(BF16)
                xs[wave, at, pl.ds(pl.multiple_of(my_start + n * chunk, chunk), chunk)] = got[:span]
                staging[at, pl.ds(n * chunk, chunk)] = got[span:]
            return carry

        lax.fori_loop(part * 4, part * 4 + 4, one, 0)
        at = pl.ds(part * 256, 256)
        return send(staging.at[at], xs.at[wave, at, pl.ds(my_start, half_width)],
                    in_send, in_recv, wave * 2 + part, twin)

    def up_projection(wave, first, count):
        at = pl.ds(first, count)

        def one(n, carry):
            cols = pl.ds(pl.multiple_of(n * n_tile, n_tile), n_tile)
            acts[at, cols] = jnp.dot(xs[wave, at], wgu[:, cols], preferred_element_type=F32)
            return carry

        lax.fori_loop(0, 2 * ff // n_tile, one, 0)

    def activate():
        def squash(i, carry):
            at = pl.ds(pl.multiple_of(i * 32, 32), 32)
            gate = acts[at, pl.ds(0, ff)]
            hidden[at] = (gate / (1.0 + jnp.exp(-gate)) * acts[at, pl.ds(ff, ff)]).astype(BF16)
            return carry

        lax.fori_loop(0, slots // 32, squash, 0)

    def down_twin(wave, part):
        quarter = half_width // 2

        def one(n, carry):
            at = part * quarter + n * n_tile
            outgoing[:, pl.ds(pl.multiple_of(at, n_tile), n_tile)] = jnp.dot(
                hidden[...], wd[:, pl.ds(pl.multiple_of(twin_start + at, n_tile), n_tile)],
                preferred_element_type=F32).astype(BF16)
            return carry

        lax.fori_loop(0, quarter // n_tile, one, 0, unroll=4)
        cols = pl.ds(part * quarter, quarter)
        return send(outgoing.at[:, cols], back.at[wave, :, cols], back_send, back_recv, wave * 2 + part, twin)

    def down_mine(wave):
        def one(n, carry):
            at = n * n_tile
            xs[wave, :, pl.ds(pl.multiple_of(at, n_tile), n_tile)] = jnp.dot(
                hidden[...], wd[:, pl.ds(pl.multiple_of(my_start + at, n_tile), n_tile)],
                preferred_element_type=F32).astype(BF16)
            return carry

        lax.fori_loop(0, half_width // n_tile, one, 0, unroll=4)

    def mix(wave, colour):
        start, size = BACK[colour]
        cols = pl.ds(start, size)

        def one(g, carry):
            at = pl.ds(g * span, span)
            both = jnp.concatenate([xs[wave, at, cols], back[wave, at, cols]], axis=0)
            got = jnp.dot(places[wave, g], both, preferred_element_type=F32).astype(BF16)
            rows[wave, g // 2, pl.ds(g % 2 * 2, 2), :, :, cols] = got.reshape(2, SIDE, tok, size)
            return carry

        for g in range(groups):
            one(g, 0)

    class Scatter:
        def __init__(self, wave):
            self.wave, self.all, self.fars, self.seconds = wave, [], [], []

        def send(self, phase, colour, n, view, landing, off):
            number = self.wave * 36 + (18 + colour * 6 + n if phase == 2 else 9 * phase + colour * 3 + n)
            copy = send(view, landing, rs_send, rs_recv, number, near((colour + phase) % 3, off))
            self.all.append(copy)
            return copy

        def land(self, ref, colour, phase, way, half):
            cols = pl.ds(*BACK[colour])
            if phase == 0:
                return ref.at[self.wave, way, :, cols]
            lead = pl.ds(0, ref.shape[2]) if half is None else pl.ds(2 * half, 2)
            if phase == 1:
                return ref.at[self.wave, way, lead, :, cols]
            return ref.at[self.wave, way, lead, :, :, cols]

        def add(self, colour, phase, at, half, ref, ways):
            cols = pl.ds(*BACK[colour])
            dims = spread_dims(colour, phase)

            def one(lead, carry):
                index = list(pos)
                index[(colour + phase) % 3] = at
                if phase == 2:
                    index[dims[1]] = pl.ds(0, SIDE)
                    index[dims[0]] = lead if half is None else lead + 2 * half
                if phase == 1:
                    index[dims[0]] = pl.ds(0, SIDE)
                here = (self.wave, index[0], index[1], index[2], slice(None), cols)
                total = rows[here].astype(F32)
                for way in ways:
                    where = (self.wave, way) + {0: (), 1: (pl.ds(0, SIDE),), 2: (lead, pl.ds(0, SIDE))}[phase]
                    total = total + ref[where + (slice(None), cols)].astype(F32)
                rows[here] = total.astype(BF16)
                return carry

            if phase == 2:
                lax.fori_loop(0, SIDE if half is None else 2, one, 0)
            else:
                one(0, 0)

        def planes(self, colour):
            for n, (off, half) in enumerate(((1, 0), (-1, 1))):
                at = step((colour + 2) % 3, 2)
                self.fars.append((colour, off, half, n, self.send(
                    2, colour, n, piece(self.wave, colour, 2, at, half, BACK),
                    self.land(ra2, colour, 2, n, None), off)))
            for n, (off, half) in enumerate(((1, 1), (-1, 0))):
                at = step((colour + 2) % 3, off)
                self.seconds.append(self.send(
                    2, colour, 2 + n, piece(self.wave, colour, 2, at, half, BACK),
                    self.land(rb2, colour, 2, n, half), off))

        def relay(self):
            for colour, off, half, n, copy in self.fars:
                copy.wait_recv()
                at = step((colour + 2) % 3, off)
                self.add(colour, 2, at, half, ra2, (n,))
                self.seconds.append(self.send(2, colour, 4 + n, piece(self.wave, colour, 2, at, half, BACK),
                                              self.land(rb2, colour, 2, n, half), off))

        def own_plane(self):
            for copy in self.seconds:
                copy.wait_recv()
            for colour in range(3):
                self.add(colour, 2, pos[(colour + 2) % 3], None, rb2, (0, 1))

        def direct(self, phase):
            ref = r1 if phase == 1 else r0
            self.last = []
            for n, off in ((2, 2), (0, 1), (1, -1)):
                for colour in range(3):
                    at = step((colour + phase) % 3, off)
                    self.last.append(self.send(phase, colour, n, piece(self.wave, colour, phase, at, None, BACK),
                                               self.land(ref, colour, phase, n, None), off))

        def settle(self, phase):
            ref = r1 if phase == 1 else r0
            for copy in self.last:
                copy.wait_recv()
            for colour in range(3):
                self.add(colour, phase, pos[(colour + phase) % 3], None, ref, (0, 1, 2))

        def drain(self):
            for copy in self.all:
                copy.wait_send()

    picked0 = [pick(0, 0)]
    g1.planes()
    picked0.append(pick(0, 1))
    loads[0].wait()
    loads[1].wait()
    picked0[0].wait()
    up_projection(0, 0, slots // 2)
    g1.relay()
    picked0[1].wait()
    up_projection(0, slots // 2, slots // 2)
    activate()
    loads[2].wait()
    sent0 = [down_twin(0, 0), down_twin(0, 1)]
    down_mine(0)
    g0.drain()
    for copy in sent0:
        copy.wait()
    s0, s1 = Scatter(0), Scatter(1)
    for colour in range(3):
        mix(0, colour)
        s0.planes(colour)
    g1.arrive()
    picked1 = [pick(1, 0), pick(1, 1)]
    picked1[0].wait()
    up_projection(1, 0, slots // 2)
    s0.relay()
    picked1[1].wait()
    up_projection(1, slots // 2, slots // 2)
    activate()
    sent1 = [down_twin(1, 0), down_twin(1, 1)]
    down_mine(1)
    s0.own_plane()
    s0.direct(1)
    g1.drain()
    for copy in sent1:
        copy.wait()
    for colour in range(3):
        mix(1, colour)
        s1.planes(colour)
    s0.settle(1)
    s0.direct(0)
    s1.relay()
    s0.settle(0)
    s1.own_plane()
    s1.direct(1)
    s1.settle(1)
    s1.direct(0)
    s1.settle(0)
    swap.wait_send()
    swap_facts.wait_send()
    ending = send(rows.at[1 - core, pos[0], pos[1], pos[2], :, body], final, swap_send, swap_recv, 1, twin)
    out_ref[:, pl.ds(my_start, half_width)] = rows[core, pos[0], pos[1], pos[2], :, body]
    s0.drain()
    s1.drain()
    ending.wait()
    out_ref[:, pl.ds(twin_start, half_width)] = final[...]


def shards(tokens, routes, router_weight, gate_weight, up_weight, down_weight):
    tok, width = tokens.shape
    half = width // 2
    ff = gate_weight.shape[2]
    cube = (WAVES, SIDE, SIDE, SIDE)
    vmem = pl.BlockSpec(memory_space=pltpu.VMEM)
    anywhere = pl.BlockSpec(memory_space=pl.ANY)
    dma = pltpu.SemaphoreType.DMA
    return pl.pallas_call(
        kernel,
        out_shape=jax.ShapeDtypeStruct((tok, width), BF16),
        in_specs=[vmem, vmem, vmem, anywhere, anywhere, anywhere],
        out_specs=vmem,
        scratch_shapes=[
            pltpu.VMEM((width, 2 * ff), BF16),
            pltpu.VMEM((ff, width), BF16),
            pltpu.VMEM(cube + (tok, half + LANES), BF16),
            pltpu.VMEM((WAVES, 8, LANES, LANES), BF16),
            pltpu.VMEM((WAVES, 512, width), BF16),
            pltpu.VMEM((512, half), BF16),
            pltpu.VMEM((512, half), BF16),
            pltpu.VMEM((512, 2 * ff), F32),
            pltpu.VMEM((512, ff), BF16),
            pltpu.VMEM((WAVES, 512, half), BF16),
            pltpu.VMEM((tok, half), BF16),
            pltpu.VMEM((WAVES, 2, 2, SIDE, tok, half), BF16),
            pltpu.VMEM((WAVES, 2, SIDE, SIDE, tok, half), BF16),
            pltpu.VMEM((WAVES, 3, SIDE, tok, half), BF16),
            pltpu.VMEM((WAVES, 3, tok, half), BF16),
            dma((3,)),
            dma((72,)), dma((72,)),
            dma((3,)), dma((3,)),
            dma((4,)), dma((4,)),
            dma((4,)), dma((4,)),
            dma((72,)), dma((72,)),
        ],
        compiler_params=pltpu.CompilerParams(
            collective_id=0, has_side_effects=True, vmem_limit_bytes=VMEM_BYTES
        ),
        cost_estimate=pl.CostEstimate(flops=2 * 3 * 1024 * width * ff, bytes_accessed=6 * ff * width,
                                      transcendentals=1024 * ff),
    )(tokens, routes.T, router_weight.T, gate_weight[0], up_weight[0], down_weight[0])


def solution(mesh):
    in_specs = (
        P(("section", "expert"), None),
        P(("section", "expert"), None),
        P(),
        P("expert", None, "section"),
        P("expert", None, "section"),
        P("expert", "section", None),
    )
    out_specs = P(("section", "expert"), None)
    return jax.shard_map(shards, mesh=mesh, in_specs=in_specs, out_specs=out_specs, check_vma=False)
```

```python
import jax
import jax.numpy as jnp
from jax import lax
from jax.experimental import pallas as pl
from jax.experimental.pallas import tpu as pltpu
from jax.sharding import PartitionSpec as P

MESH = pl.DeviceIdType.MESH
F32, BF16 = jnp.float32, jnp.bfloat16
SIDE = 4
WAVES = 2
FORTH = ((0, 768), (768, 768), (1536, 640))
BACK = ((0, 768), (768, 640), (1408, 640))
LANES = 128
VMEM_BYTES = 64 * 1024 * 1024 - 65536
OFFSETS = (1, -1, 2)


def spread_dims(colour, phase):
    return sorted((colour + j) % 3 for j in range(phase))


def kernel(x_ref, routes_ref, router_ref, wg_ref, wu_ref, wd_ref, out_ref,
           wgu, wd, rows, places, xs, staging, outgoing, acts, hidden, back, final,
           ra2, rb2, r1, r0,
           w_sem, ag_send, ag_recv, swap_send, swap_recv, in_send, in_recv,
           back_send, back_recv, rs_send, rs_recv):
    section, expert = lax.axis_index("section"), lax.axis_index("expert")
    core = lax.rem(expert, 2)
    pos = [lax.div(section, SIDE), lax.div(expert, 2), lax.rem(section, SIDE)]
    tok, width = x_ref.shape
    half_width = width // 2
    ff = wg_ref.shape[1]
    other_expert = pos[1] * 2 + 1 - core
    twin = (section, other_expert)
    my_start = pl.multiple_of(core * half_width, half_width)
    twin_start = pl.multiple_of((1 - core) * half_width, half_width)

    def step(dim, off):
        return lax.rem(pos[dim] + off + SIDE, SIDE)

    def near(dim, off):
        p = list(pos)
        p[dim] = step(dim, off)
        return (p[0] * SIDE + p[2], p[1] * 2 + core)

    loads = [
        pltpu.make_async_copy(wg_ref, wgu.at[:, pl.ds(0, ff)], w_sem.at[0]),
        pltpu.make_async_copy(wu_ref, wgu.at[:, pl.ds(ff, ff)], w_sem.at[1]),
        pltpu.make_async_copy(wd_ref, wd, w_sem.at[2]),
    ]

    barrier = pltpu.get_barrier_semaphore()
    greeted = [near(d, o) for d in range(3) for o in OFFSETS] + [twin]
    for device in greeted:
        pl.semaphore_signal(barrier, inc=1, device_id=device, device_id_type=MESH)
    for load in loads:
        load.start()

    body = pl.ds(0, half_width)
    tail = pl.ds(half_width, LANES)
    rows[core, pos[0], pos[1], pos[2], :, body] = x_ref[:, pl.ds(my_start, half_width)]

    logits = lax.dot_general(x_ref[...], router_ref[...], (((1,), (1,)), ((), ())),
                             preferred_element_type=F32)
    square = (tok, tok)
    down_rows, over_lanes = lax.broadcasted_iota(jnp.int32, square, 0), lax.broadcasted_iota(jnp.int32, square, 1)

    def upright(k):
        spread = jnp.broadcast_to(routes_ref[k:k + 1, :], square)
        return jnp.sum(jnp.where(down_rows == over_lanes, spread, 0), axis=1, keepdims=True)

    first, second = upright(0), upright(1)
    narrow = lax.broadcasted_iota(jnp.int32, logits.shape, 1)
    gap = (jnp.sum(jnp.where(narrow == first, logits, 0.0), axis=1, keepdims=True)
           - jnp.sum(jnp.where(narrow == second, logits, 0.0), axis=1, keepdims=True))
    gate0 = jax.nn.sigmoid(gap)
    gate1 = 1.0 - gate0
    lane = lax.broadcasted_iota(jnp.int32, (tok, LANES), 1)
    named = jnp.where(lane == first, 1.0, 0.0) + jnp.where(lane == second, 1.0, 0.0)
    below = jnp.where(down_rows > over_lanes, 1.0, 0.0)
    earlier = jnp.dot(below.astype(BF16), named.astype(BF16), preferred_element_type=F32)
    facts = (named * (earlier + 1.0) + jnp.where(lane == first + 8, gate0, 0.0)
             + jnp.where(lane == second + 8, gate1, 0.0))
    rows[core, pos[0], pos[1], pos[2], :, tail] = facts.astype(BF16)

    def send(src, dst, sends, recvs, n, device):
        copy = pltpu.make_async_remote_copy(src_ref=src, dst_ref=dst, send_sem=sends.at[n], recv_sem=recvs.at[n],
                                            device_id=device, device_id_type=MESH)
        copy.start()
        return copy

    pl.semaphore_wait(barrier, len(greeted))
    swap = send(x_ref.at[:, pl.ds(twin_start, half_width)], rows.at[core, pos[0], pos[1], pos[2], :, body],
                swap_send, swap_recv, 0, twin)

    own_facts = rows.at[core, pos[0], pos[1], pos[2], :, tail]
    swap_facts = send(own_facts, own_facts, swap_send, swap_recv, 2, twin)

    def piece(wave, colour, phase, at, half, colours):
        start, size = colours[colour]
        index = list(pos)
        index[(colour + phase) % 3] = at
        for n, d in enumerate(spread_dims(colour, phase)):
            index[d] = pl.ds(0, SIDE) if n or half is None else pl.ds(2 * half, 2)
        return rows.at[wave, index[0], index[1], index[2], :, pl.ds(start, size)]

    class Gather:
        def __init__(self, wave):
            self.wave, self.all, self.last = wave, [], []

        def number(self, phase, colour, n):
            return self.wave * 36 + (colour * 3 + n if phase < 2 else 18 + colour * 6 + n) + 9 * (phase == 1)

        def send(self, phase, colour, n, view, off):
            copy = send(view, view, ag_send, ag_recv, self.number(phase, colour, n), near((colour + phase) % 3, off))
            self.all.append(copy)
            return copy

        def arrive(self):
            for copy in self.last:
                copy.wait_recv()

        def direct(self, phase):
            self.arrive()
            self.last = []
            for n, off in enumerate(OFFSETS):
                for colour in range(3):
                    view = piece(self.wave, colour, phase, pos[(colour + phase) % 3], None, FORTH)
                    self.last.append(self.send(phase, colour, n, view, off))

        def planes(self):
            self.arrive()
            self.last, self.relayed = [], []
            for n, (off, half) in enumerate(((1, 0), (-1, 1), (1, 1), (-1, 0))):
                for colour in range(3):
                    view = piece(self.wave, colour, 2, pos[(colour + 2) % 3], half, FORTH)
                    copy = self.send(2, colour, n, view, off)
                    (self.relayed if n < 2 else self.last).append((colour, off, half, copy) if n < 2 else copy)

        def relay(self):
            for n, (colour, off, half, copy) in enumerate(self.relayed):
                copy.wait_recv()
                view = piece(self.wave, colour, 2, step((colour + 2) % 3, -off), half, FORTH)
                self.last.append(self.send(2, colour, 4 + n // 3, view, off))

        def drain(self):
            for copy in self.all:
                copy.wait_send()

    swap.wait_recv()
    swap_facts.wait_recv()
    g0, g1 = Gather(0), Gather(1)
    g0.direct(0)
    g1.direct(0)
    g0.direct(1)
    g1.direct(1)
    g0.planes()
    g0.relay()
    g0.arrive()

    groups = 8
    span = 64
    wide = lax.broadcasted_iota(jnp.int32, (LANES, LANES), 1)
    tall = lax.broadcasted_iota(jnp.int32, (LANES, LANES), 0)
    block_of = (lax.div(tall, tok) * 8).astype(F32)[:, 0:1]
    wide_f = wide.astype(F32)

    def placing(wave, g):
        facts = rows[wave, lax.div(g, 2), pl.ds(lax.rem(g, 2) * 2, 2), :, :, tail].reshape(LANES, LANES).astype(F32)
        plain = jnp.zeros((LANES, LANES), F32)
        weighted = jnp.zeros((LANES, LANES), F32)
        for which, base in ((expert, 0.0), (other_expert, float(span))):
            slot = jnp.sum(jnp.where(wide == which, facts, 0.0), axis=1, keepdims=True)
            gate = jnp.sum(jnp.where(wide == which + 8, facts, 0.0), axis=1, keepdims=True)
            hit = wide_f == jnp.where(slot > 0.5, block_of + slot + (base - 1.0), -1.0)
            plain = jnp.where(hit, 1.0, plain)
            weighted = jnp.where(hit, gate, weighted)
        places[wave, g] = weighted.astype(BF16)
        return plain.astype(BF16)

    chunk = 1024
    n_tile = 256
    up_tile = 896
    tile = 256
    slots = groups * span

    def pick(wave, part):
        def one(g, carry):
            place = placing(wave, g)
            at = pl.ds(pl.multiple_of(g * span, span), span)
            for n in range(half_width // chunk):
                block = rows[wave, lax.div(g, 2), pl.ds(lax.rem(g, 2) * 2, 2), :, :, pl.ds(n * chunk, chunk)]
                got = lax.dot_general(place, block.reshape(LANES, chunk), (((0,), (0,)), ((), ())),
                                      preferred_element_type=F32).astype(BF16)
                xs[wave, at, pl.ds(pl.multiple_of(my_start + n * chunk, chunk), chunk)] = got[:span]
                staging[at, pl.ds(n * chunk, chunk)] = got[span:]
            return carry

        lax.fori_loop(part * 4, part * 4 + 4, one, 0)
        at = pl.ds(part * 256, 256)
        return send(staging.at[at], xs.at[wave, at, pl.ds(my_start, half_width)],
                    in_send, in_recv, wave * 2 + part, twin)

    def up_projection(wave, start, fresh):
        deep = pl.ds(start, half_width)

        def one(n, carry):
            cols = pl.ds(pl.multiple_of(n * up_tile, LANES), up_tile)
            part = jnp.dot(xs[wave, :, deep], wgu[deep, cols], preferred_element_type=F32)
            acts[:, cols] = part if fresh else acts[:, cols] + part
            return carry

        lax.fori_loop(0, 2 * ff // up_tile, one, 0)

    def activate():
        def squash(i, carry):
            at = pl.ds(pl.multiple_of(i * 32, 32), 32)
            gate = acts[at, pl.ds(0, ff)]
            hidden[at] = (gate / (1.0 + jnp.exp(-gate)) * acts[at, pl.ds(ff, ff)]).astype(BF16)
            return carry

        lax.fori_loop(0, slots // 32, squash, 0)

    def down_twin(wave, part):
        quarter = half_width // 2

        def one(n, carry):
            at = part * quarter + n * n_tile
            outgoing[:, pl.ds(pl.multiple_of(at, n_tile), n_tile)] = jnp.dot(
                hidden[...], wd[:, pl.ds(pl.multiple_of(twin_start + at, n_tile), n_tile)],
                preferred_element_type=F32).astype(BF16)
            return carry

        lax.fori_loop(0, quarter // n_tile, one, 0, unroll=4)
        cols = pl.ds(part * quarter, quarter)
        return send(outgoing.at[:, cols], back.at[wave, :, cols], back_send, back_recv, wave * 2 + part, twin)

    def down_mine(wave):
        def one(n, carry):
            at = n * n_tile
            xs[wave, :, pl.ds(pl.multiple_of(at, n_tile), n_tile)] = jnp.dot(
                hidden[...], wd[:, pl.ds(pl.multiple_of(my_start + at, n_tile), n_tile)],
                preferred_element_type=F32).astype(BF16)
            return carry

        lax.fori_loop(0, half_width // n_tile, one, 0, unroll=4)

    def mix(wave, colour):
        start, size = BACK[colour]
        cols = pl.ds(start, size)

        def one(g, carry):
            at = pl.ds(g * span, span)
            both = jnp.concatenate([xs[wave, at, cols], back[wave, at, cols]], axis=0)
            got = jnp.dot(places[wave, g], both, preferred_element_type=F32).astype(BF16)
            rows[wave, g // 2, pl.ds(g % 2 * 2, 2), :, :, cols] = got.reshape(2, SIDE, tok, size)
            return carry

        for g in range(groups):
            one(g, 0)

    class Scatter:
        def __init__(self, wave):
            self.wave, self.all, self.fars, self.seconds = wave, [], [], []

        def send(self, phase, colour, n, view, landing, off):
            number = self.wave * 36 + (18 + colour * 6 + n if phase == 2 else 9 * phase + colour * 3 + n)
            copy = send(view, landing, rs_send, rs_recv, number, near((colour + phase) % 3, off))
            self.all.append(copy)
            return copy

        def land(self, ref, colour, phase, way, half):
            cols = pl.ds(*BACK[colour])
            if phase == 0:
                return ref.at[self.wave, way, :, cols]
            lead = pl.ds(0, ref.shape[2]) if half is None else pl.ds(2 * half, 2)
            if phase == 1:
                return ref.at[self.wave, way, lead, :, cols]
            return ref.at[self.wave, way, lead, :, :, cols]

        def add(self, colour, phase, at, half, ref, ways):
            cols = pl.ds(*BACK[colour])
            dims = spread_dims(colour, phase)

            def one(lead, carry):
                index = list(pos)
                index[(colour + phase) % 3] = at
                if phase == 2:
                    index[dims[1]] = pl.ds(0, SIDE)
                    index[dims[0]] = lead if half is None else lead + 2 * half
                if phase == 1:
                    index[dims[0]] = pl.ds(0, SIDE)
                here = (self.wave, index[0], index[1], index[2], slice(None), cols)
                total = rows[here].astype(F32)
                for way in ways:
                    where = (self.wave, way) + {0: (), 1: (pl.ds(0, SIDE),), 2: (lead, pl.ds(0, SIDE))}[phase]
                    total = total + ref[where + (slice(None), cols)].astype(F32)
                rows[here] = total.astype(BF16)
                return carry

            if phase == 2:
                lax.fori_loop(0, SIDE if half is None else 2, one, 0)
            else:
                one(0, 0)

        def planes(self, colour):
            for n, (off, half) in enumerate(((1, 0), (-1, 1))):
                at = step((colour + 2) % 3, 2)
                self.fars.append((colour, off, half, n, self.send(
                    2, colour, n, piece(self.wave, colour, 2, at, half, BACK),
                    self.land(ra2, colour, 2, n, None), off)))
            for n, (off, half) in enumerate(((1, 1), (-1, 0))):
                at = step((colour + 2) % 3, off)
                self.seconds.append((colour, self.send(
                    2, colour, 2 + n, piece(self.wave, colour, 2, at, half, BACK),
                    self.land(rb2, colour, 2, n, half), off)))

        def relay(self):
            for colour, off, half, n, copy in self.fars:
                copy.wait_recv()
                at = step((colour + 2) % 3, off)
                self.add(colour, 2, at, half, ra2, (n,))
                self.seconds.append((colour, self.send(
                    2, colour, 4 + n, piece(self.wave, colour, 2, at, half, BACK),
                    self.land(rb2, colour, 2, n, half), off)))

        def lines(self):
            self.last = []
            for colour in (2, 1, 0):
                for copy in self.seconds:
                    if copy[0] == colour:
                        copy[1].wait_recv()
                self.add(colour, 2, pos[(colour + 2) % 3], None, rb2, (0, 1))
                self.direct(1, colour)

        def points(self):
            lines, self.last = self.last, []
            for colour in (2, 1, 0):
                self.settle(1, colour, lines)
                self.direct(0, colour)

        def finish(self):
            for colour in (2, 1, 0):
                self.settle(0, colour, self.last)

        def direct(self, phase, colour):
            ref = r1 if phase == 1 else r0
            for n, off in ((2, 2), (0, 1), (1, -1)):
                at = step((colour + phase) % 3, off)
                self.last.append((colour, self.send(
                    phase, colour, n, piece(self.wave, colour, phase, at, None, BACK),
                    self.land(ref, colour, phase, n, None), off)))

        def settle(self, phase, colour, copies):
            for which, copy in copies:
                if which == colour:
                    copy.wait_recv()
            ref = r1 if phase == 1 else r0
            self.add(colour, phase, pos[(colour + phase) % 3], None, ref, (0, 1, 2))

        def drain(self):
            for copy in self.all:
                copy.wait_send()

    picked0 = [pick(0, 0)]
    g1.planes()
    picked0.append(pick(0, 1))
    loads[0].wait()
    loads[1].wait()
    up_projection(0, my_start, True)
    for copy in picked0:
        copy.wait()
    g1.relay()
    up_projection(0, twin_start, False)
    activate()
    loads[2].wait()
    sent0 = [down_twin(0, 0), down_twin(0, 1)]
    down_mine(0)
    g0.drain()
    for copy in sent0:
        copy.wait()
    s0, s1 = Scatter(0), Scatter(1)
    for colour in range(3):
        mix(0, colour)
        s0.planes(colour)
    g1.arrive()
    picked1 = [pick(1, 0), pick(1, 1)]
    up_projection(1, my_start, True)
    for copy in picked1:
        copy.wait()
    s0.relay()
    up_projection(1, twin_start, False)
    activate()
    sent1 = [down_twin(1, 0), down_twin(1, 1)]
    down_mine(1)
    s0.lines()
    g1.drain()
    for copy in sent1:
        copy.wait()
    for colour in range(3):
        mix(1, colour)
        s1.planes(colour)
    s1.relay()
    s0.points()
    s1.lines()
    s0.finish()
    s1.points()
    s1.finish()
    swap.wait_send()
    swap_facts.wait_send()
    ending = send(rows.at[1 - core, pos[0], pos[1], pos[2], :, body], final, swap_send, swap_recv, 1, twin)
    out_ref[:, pl.ds(my_start, half_width)] = rows[core, pos[0], pos[1], pos[2], :, body]
    s0.drain()
    s1.drain()
    ending.wait()
    out_ref[:, pl.ds(twin_start, half_width)] = final[...]


def shards(tokens, routes, router_weight, gate_weight, up_weight, down_weight):
    tok, width = tokens.shape
    half = width // 2
    ff = gate_weight.shape[2]
    cube = (WAVES, SIDE, SIDE, SIDE)
    vmem = pl.BlockSpec(memory_space=pltpu.VMEM)
    anywhere = pl.BlockSpec(memory_space=pl.ANY)
    dma = pltpu.SemaphoreType.DMA
    return pl.pallas_call(
        kernel,
        out_shape=jax.ShapeDtypeStruct((tok, width), BF16),
        in_specs=[vmem, vmem, vmem, anywhere, anywhere, anywhere],
        out_specs=vmem,
        scratch_shapes=[
            pltpu.VMEM((width, 2 * ff), BF16),
            pltpu.VMEM((ff, width), BF16),
            pltpu.VMEM(cube + (tok, half + LANES), BF16),
            pltpu.VMEM((WAVES, 8, LANES, LANES), BF16),
            pltpu.VMEM((WAVES, 512, width), BF16),
            pltpu.VMEM((512, half), BF16),
            pltpu.VMEM((512, half), BF16),
            pltpu.VMEM((512, 2 * ff), F32),
            pltpu.VMEM((512, ff), BF16),
            pltpu.VMEM((WAVES, 512, half), BF16),
            pltpu.VMEM((tok, half), BF16),
            pltpu.VMEM((WAVES, 2, 2, SIDE, tok, half), BF16),
            pltpu.VMEM((WAVES, 2, SIDE, SIDE, tok, half), BF16),
            pltpu.VMEM((WAVES, 3, SIDE, tok, half), BF16),
            pltpu.VMEM((WAVES, 3, tok, half), BF16),
            dma((3,)),
            dma((72,)), dma((72,)),
            dma((3,)), dma((3,)),
            dma((4,)), dma((4,)),
            dma((4,)), dma((4,)),
            dma((72,)), dma((72,)),
        ],
        compiler_params=pltpu.CompilerParams(
            collective_id=0, has_side_effects=True, vmem_limit_bytes=VMEM_BYTES
        ),
        cost_estimate=pl.CostEstimate(flops=2 * 3 * 1024 * width * ff, bytes_accessed=6 * ff * width,
                                      transcendentals=1024 * ff),
    )(tokens, routes.T, router_weight.T, gate_weight[0], up_weight[0], down_weight[0])


def solution(mesh):
    in_specs = (
        P(("section", "expert"), None),
        P(("section", "expert"), None),
        P(),
        P("expert", None, "section"),
        P("expert", None, "section"),
        P("expert", "section", None),
    )
    out_specs = P(("section", "expert"), None)
    return jax.shard_map(shards, mesh=mesh, in_specs=in_specs, out_specs=out_specs, check_vma=False)
```

```python
import jax
import jax.numpy as jnp
from jax import lax
from jax.experimental import pallas as pl
from jax.experimental.pallas import tpu as pltpu
from jax.sharding import PartitionSpec as P

MESH = pl.DeviceIdType.MESH
F32, BF16 = jnp.float32, jnp.bfloat16
SIDE = 4
WAVES = 2
FORTH = ((0, 768), (768, 768), (1536, 640))
BACK = ((0, 768), (768, 640), (1408, 640))
LANES = 128
VMEM_BYTES = 64 * 1024 * 1024 - 65536
OFFSETS = (1, -1, 2)


def spread_dims(colour, phase):
    return sorted((colour + j) % 3 for j in range(phase))


def kernel(x_ref, routes_ref, router_ref, wg_ref, wu_ref, wd_ref, out_ref,
           wgu, wd, rows, places, xs, staging, outgoing, acts, hidden, back, final,
           ra2, rb2, r1, r0,
           w_sem, ag_send, ag_recv, swap_send, swap_recv, in_send, in_recv,
           back_send, back_recv, rs_send, rs_recv):
    section, expert = lax.axis_index("section"), lax.axis_index("expert")
    core = lax.rem(expert, 2)
    pos = [lax.div(section, SIDE), lax.div(expert, 2), lax.rem(section, SIDE)]
    tok, width = x_ref.shape
    half_width = width // 2
    ff = wg_ref.shape[1]
    other_expert = pos[1] * 2 + 1 - core
    twin = (section, other_expert)
    my_start = pl.multiple_of(core * half_width, half_width)
    twin_start = pl.multiple_of((1 - core) * half_width, half_width)

    def step(dim, off):
        return lax.rem(pos[dim] + off + SIDE, SIDE)

    def near(dim, off):
        p = list(pos)
        p[dim] = step(dim, off)
        return (p[0] * SIDE + p[2], p[1] * 2 + core)

    loads = [
        pltpu.make_async_copy(wg_ref, wgu.at[:, pl.ds(0, ff)], w_sem.at[0]),
        pltpu.make_async_copy(wu_ref, wgu.at[:, pl.ds(ff, ff)], w_sem.at[1]),
        pltpu.make_async_copy(wd_ref, wd, w_sem.at[2]),
    ]

    barrier = pltpu.get_barrier_semaphore()
    greeted = [near(d, o) for d in range(3) for o in OFFSETS] + [twin]
    for device in greeted:
        pl.semaphore_signal(barrier, inc=1, device_id=device, device_id_type=MESH)
    for load in loads:
        load.start()

    body = pl.ds(0, half_width)
    tail = pl.ds(half_width, LANES)
    rows[core, pos[0], pos[1], pos[2], :, body] = x_ref[:, pl.ds(my_start, half_width)]

    logits = lax.dot_general(x_ref[...], router_ref[...], (((1,), (1,)), ((), ())),
                             preferred_element_type=F32)
    square = (tok, tok)
    down_rows, over_lanes = lax.broadcasted_iota(jnp.int32, square, 0), lax.broadcasted_iota(jnp.int32, square, 1)

    def upright(k):
        spread = jnp.broadcast_to(routes_ref[k:k + 1, :], square)
        return jnp.sum(jnp.where(down_rows == over_lanes, spread, 0), axis=1, keepdims=True)

    first, second = upright(0), upright(1)
    narrow = lax.broadcasted_iota(jnp.int32, logits.shape, 1)
    gap = (jnp.sum(jnp.where(narrow == first, logits, 0.0), axis=1, keepdims=True)
           - jnp.sum(jnp.where(narrow == second, logits, 0.0), axis=1, keepdims=True))
    gate0 = jax.nn.sigmoid(gap)
    gate1 = 1.0 - gate0
    lane = lax.broadcasted_iota(jnp.int32, (tok, LANES), 1)
    named = jnp.where(lane == first, 1.0, 0.0) + jnp.where(lane == second, 1.0, 0.0)
    below = jnp.where(down_rows > over_lanes, 1.0, 0.0)
    earlier = jnp.dot(below.astype(BF16), named.astype(BF16), preferred_element_type=F32)
    facts = (named * (earlier + 1.0) + jnp.where(lane == first + 8, gate0, 0.0)
             + jnp.where(lane == second + 8, gate1, 0.0))
    rows[core, pos[0], pos[1], pos[2], :, tail] = facts.astype(BF16)

    def send(src, dst, sends, recvs, n, device):
        copy = pltpu.make_async_remote_copy(src_ref=src, dst_ref=dst, send_sem=sends.at[n], recv_sem=recvs.at[n],
                                            device_id=device, device_id_type=MESH)
        copy.start()
        return copy

    pl.semaphore_wait(barrier, len(greeted))
    swap = send(x_ref.at[:, pl.ds(twin_start, half_width)], rows.at[core, pos[0], pos[1], pos[2], :, body],
                swap_send, swap_recv, 0, twin)

    own_facts = rows.at[core, pos[0], pos[1], pos[2], :, tail]
    swap_facts = send(own_facts, own_facts, swap_send, swap_recv, 2, twin)

    def piece(wave, colour, phase, at, half, colours):
        start, size = colours[colour]
        index = list(pos)
        index[(colour + phase) % 3] = at
        for n, d in enumerate(spread_dims(colour, phase)):
            index[d] = pl.ds(0, SIDE) if n or half is None else pl.ds(2 * half, 2)
        return rows.at[wave, index[0], index[1], index[2], :, pl.ds(start, size)]

    class Gather:
        def __init__(self, wave):
            self.wave, self.all, self.last = wave, [], []

        def number(self, phase, colour, n):
            return self.wave * 36 + (colour * 3 + n if phase < 2 else 18 + colour * 6 + n) + 9 * (phase == 1)

        def send(self, phase, colour, n, view, off):
            copy = send(view, view, ag_send, ag_recv, self.number(phase, colour, n), near((colour + phase) % 3, off))
            self.all.append(copy)
            return copy

        def arrive(self, only=None):
            for colour, copy in self.last:
                if only is None or colour == only:
                    copy.wait_recv()

        def direct(self, phase):
            now = []
            for colour in range(3):
                self.arrive(colour)
                for n, off in ((2, 2), (0, 1), (1, -1)):
                    view = piece(self.wave, colour, phase, pos[(colour + phase) % 3], None, FORTH)
                    now.append((colour, self.send(phase, colour, n, view, off)))
            self.last = now

        def planes(self):
            now, self.relayed = [], []
            for colour in range(3):
                self.arrive(colour)
                for n, (off, half) in enumerate(((1, 0), (-1, 1), (1, 1), (-1, 0))):
                    view = piece(self.wave, colour, 2, pos[(colour + 2) % 3], half, FORTH)
                    copy = self.send(2, colour, n, view, off)
                    if n < 2:
                        self.relayed.append((n, colour, off, half, copy))
                    else:
                        now.append((colour, copy))
            self.last = now

        def relay(self):
            for n, colour, off, half, copy in self.relayed:
                copy.wait_recv()
                view = piece(self.wave, colour, 2, step((colour + 2) % 3, -off), half, FORTH)
                self.last.append((colour, self.send(2, colour, 4 + n, view, off)))

        def drain(self):
            for copy in self.all:
                copy.wait_send()

    swap.wait_recv()
    swap_facts.wait_recv()
    g0, g1 = Gather(0), Gather(1)
    g0.direct(0)
    g1.direct(0)
    g0.direct(1)
    g1.direct(1)
    g0.planes()
    g0.relay()
    g0.arrive()

    groups = 8
    span = 64
    wide = lax.broadcasted_iota(jnp.int32, (LANES, LANES), 1)
    tall = lax.broadcasted_iota(jnp.int32, (LANES, LANES), 0)
    block_of = (lax.div(tall, tok) * 8).astype(F32)[:, 0:1]
    wide_f = wide.astype(F32)

    def placing(wave, g):
        facts = rows[wave, g // 2, pl.ds(g % 2 * 2, 2), :, :, tail].reshape(LANES, LANES).astype(F32)
        plain = jnp.zeros((LANES, LANES), F32)
        weighted = jnp.zeros((LANES, LANES), F32)
        for which, base in ((expert, 0.0), (other_expert, float(span))):
            slot = jnp.sum(jnp.where(wide == which, facts, 0.0), axis=1, keepdims=True)
            gate = jnp.sum(jnp.where(wide == which + 8, facts, 0.0), axis=1, keepdims=True)
            hit = wide_f == jnp.where(slot > 0.5, block_of + slot + (base - 1.0), -1.0)
            plain = jnp.where(hit, 1.0, plain)
            weighted = jnp.where(hit, gate, weighted)
        places[wave, g] = weighted.astype(BF16)
        return plain.astype(BF16)

    chunk = 1024
    n_tile = 256
    up_tile = 896
    tile = 256
    slots = groups * span

    def pick(wave, part):
        def one(g, carry):
            place = placing(wave, g)
            at = pl.ds(g * span, span)
            for n in range(half_width // chunk):
                block = rows[wave, g // 2, pl.ds(g % 2 * 2, 2), :, :, pl.ds(n * chunk, chunk)]
                got = lax.dot_general(place, block.reshape(LANES, chunk), (((0,), (0,)), ((), ())),
                                      preferred_element_type=F32).astype(BF16)
                xs[wave, at, pl.ds(pl.multiple_of(my_start + n * chunk, chunk), chunk)] = got[:span]
                staging[at, pl.ds(n * chunk, chunk)] = got[span:]
            return carry

        for g in range(part * 4, part * 4 + 4):
            one(g, 0)
        at = pl.ds(part * 256, 256)
        return send(staging.at[at], xs.at[wave, at, pl.ds(my_start, half_width)],
                    in_send, in_recv, wave * 2 + part, twin)

    def up_projection(wave, start, fresh):
        deep = pl.ds(start, half_width)

        def one(n, carry):
            cols = pl.ds(pl.multiple_of(n * up_tile, LANES), up_tile)
            part = jnp.dot(xs[wave, :, deep], wgu[deep, cols], preferred_element_type=F32)
            acts[:, cols] = part if fresh else acts[:, cols] + part
            return carry

        lax.fori_loop(0, 2 * ff // up_tile, one, 0)

    def activate():
        def squash(i, carry):
            at = pl.ds(pl.multiple_of(i * 32, 32), 32)
            gate = acts[at, pl.ds(0, ff)]
            hidden[at] = (gate / (1.0 + jnp.exp(-gate)) * acts[at, pl.ds(ff, ff)]).astype(BF16)
            return carry

        lax.fori_loop(0, slots // 32, squash, 0)

    def down_twin(wave, part):
        quarter = half_width // 2

        def one(n, carry):
            at = part * quarter + n * n_tile
            outgoing[:, pl.ds(pl.multiple_of(at, n_tile), n_tile)] = jnp.dot(
                hidden[...], wd[:, pl.ds(pl.multiple_of(twin_start + at, n_tile), n_tile)],
                preferred_element_type=F32).astype(BF16)
            return carry

        lax.fori_loop(0, quarter // n_tile, one, 0, unroll=4)
        cols = pl.ds(part * quarter, quarter)
        return send(outgoing.at[:, cols], back.at[wave, :, cols], back_send, back_recv, wave * 2 + part, twin)

    def down_mine(wave):
        def one(n, carry):
            at = n * n_tile
            xs[wave, :, pl.ds(pl.multiple_of(at, n_tile), n_tile)] = jnp.dot(
                hidden[...], wd[:, pl.ds(pl.multiple_of(my_start + at, n_tile), n_tile)],
                preferred_element_type=F32).astype(BF16)
            return carry

        lax.fori_loop(0, half_width // n_tile, one, 0, unroll=4)

    def mix(wave, colour):
        start, size = BACK[colour]
        cols = pl.ds(start, size)

        def one(g, carry):
            at = pl.ds(g * span, span)
            both = jnp.concatenate([xs[wave, at, cols], back[wave, at, cols]], axis=0)
            got = jnp.dot(places[wave, g], both, preferred_element_type=F32).astype(BF16)
            rows[wave, g // 2, pl.ds(g % 2 * 2, 2), :, :, cols] = got.reshape(2, SIDE, tok, size)
            return carry

        for g in range(groups):
            one(g, 0)

    class Scatter:
        def __init__(self, wave):
            self.wave, self.all, self.fars, self.seconds = wave, [], [], []

        def send(self, phase, colour, n, view, landing, off):
            number = self.wave * 36 + (18 + colour * 6 + n if phase == 2 else 9 * phase + colour * 3 + n)
            copy = send(view, landing, rs_send, rs_recv, number, near((colour + phase) % 3, off))
            self.all.append(copy)
            return copy

        def land(self, ref, colour, phase, way, half):
            cols = pl.ds(*BACK[colour])
            if phase == 0:
                return ref.at[self.wave, way, :, cols]
            lead = pl.ds(0, ref.shape[2]) if half is None else pl.ds(2 * half, 2)
            if phase == 1:
                return ref.at[self.wave, way, lead, :, cols]
            return ref.at[self.wave, way, lead, :, :, cols]

        def add(self, colour, phase, at, half, ref, ways):
            cols = pl.ds(*BACK[colour])
            dims = spread_dims(colour, phase)

            def one(lead, carry):
                index = list(pos)
                index[(colour + phase) % 3] = at
                if phase == 2:
                    index[dims[1]] = pl.ds(0, SIDE)
                    index[dims[0]] = lead if half is None else lead + 2 * half
                if phase == 1:
                    index[dims[0]] = pl.ds(0, SIDE)
                here = (self.wave, index[0], index[1], index[2], slice(None), cols)
                total = rows[here].astype(F32)
                for way in ways:
                    where = (self.wave, way) + {0: (), 1: (pl.ds(0, SIDE),), 2: (lead, pl.ds(0, SIDE))}[phase]
                    total = total + ref[where + (slice(None), cols)].astype(F32)
                rows[here] = total.astype(BF16)
                return carry

            if phase == 2:
                lax.fori_loop(0, SIDE if half is None else 2, one, 0)
            else:
                one(0, 0)

        def planes(self, colour):
            for n, (off, half) in enumerate(((1, 0), (-1, 1))):
                at = step((colour + 2) % 3, 2)
                self.fars.append((colour, off, half, n, self.send(
                    2, colour, n, piece(self.wave, colour, 2, at, half, BACK),
                    self.land(ra2, colour, 2, n, None), off)))
            for n, (off, half) in enumerate(((1, 1), (-1, 0))):
                at = step((colour + 2) % 3, off)
                self.seconds.append((colour, self.send(
                    2, colour, 2 + n, piece(self.wave, colour, 2, at, half, BACK),
                    self.land(rb2, colour, 2, n, half), off)))

        def relay(self):
            for colour, off, half, n, copy in self.fars:
                copy.wait_recv()
                at = step((colour + 2) % 3, off)
                self.add(colour, 2, at, half, ra2, (n,))
                self.seconds.append((colour, self.send(
                    2, colour, 4 + n, piece(self.wave, colour, 2, at, half, BACK),
                    self.land(rb2, colour, 2, n, half), off)))

        def lines(self):
            self.last = []
            for colour in (2, 1, 0):
                for copy in self.seconds:
                    if copy[0] == colour:
                        copy[1].wait_recv()
                self.add(colour, 2, pos[(colour + 2) % 3], None, rb2, (0, 1))
                self.direct(1, colour)

        def points(self):
            lines, self.last = self.last, []
            for colour in (2, 1, 0):
                self.settle(1, colour, lines)
                self.direct(0, colour)

        def finish(self):
            for colour in (2, 1, 0):
                self.settle(0, colour, self.last)

        def direct(self, phase, colour):
            ref = r1 if phase == 1 else r0
            for n, off in ((2, 2), (0, 1), (1, -1)):
                at = step((colour + phase) % 3, off)
                self.last.append((colour, self.send(
                    phase, colour, n, piece(self.wave, colour, phase, at, None, BACK),
                    self.land(ref, colour, phase, n, None), off)))

        def settle(self, phase, colour, copies):
            for which, copy in copies:
                if which == colour:
                    copy.wait_recv()
            ref = r1 if phase == 1 else r0
            self.add(colour, phase, pos[(colour + phase) % 3], None, ref, (0, 1, 2))

        def drain(self):
            for copy in self.all:
                copy.wait_send()

    picked0 = [pick(0, 0)]
    g1.planes()
    picked0.append(pick(0, 1))
    loads[0].wait()
    loads[1].wait()
    up_projection(0, my_start, True)
    for copy in picked0:
        copy.wait()
    g1.relay()
    up_projection(0, twin_start, False)
    activate()
    loads[2].wait()
    sent0 = [down_twin(0, 0), down_twin(0, 1)]
    down_mine(0)
    g0.drain()
    for copy in sent0:
        copy.wait()
    s0, s1 = Scatter(0), Scatter(1)
    for colour in range(3):
        mix(0, colour)
        s0.planes(colour)
    g1.arrive()
    picked1 = [pick(1, 0), pick(1, 1)]
    up_projection(1, my_start, True)
    for copy in picked1:
        copy.wait()
    s0.relay()
    up_projection(1, twin_start, False)
    activate()
    sent1 = [down_twin(1, 0), down_twin(1, 1)]
    down_mine(1)
    s0.lines()
    g1.drain()
    for copy in sent1:
        copy.wait()
    for colour in range(3):
        mix(1, colour)
        s1.planes(colour)
    s1.relay()
    s0.points()
    s1.lines()
    s0.finish()
    s1.points()
    s1.finish()
    swap.wait_send()
    swap_facts.wait_send()
    ending = send(rows.at[1 - core, pos[0], pos[1], pos[2], :, body], final, swap_send, swap_recv, 1, twin)
    out_ref[:, pl.ds(my_start, half_width)] = rows[core, pos[0], pos[1], pos[2], :, body]
    s0.drain()
    s1.drain()
    ending.wait()
    out_ref[:, pl.ds(twin_start, half_width)] = final[...]


def shards(tokens, routes, router_weight, gate_weight, up_weight, down_weight):
    tok, width = tokens.shape
    half = width // 2
    ff = gate_weight.shape[2]
    cube = (WAVES, SIDE, SIDE, SIDE)
    vmem = pl.BlockSpec(memory_space=pltpu.VMEM)
    anywhere = pl.BlockSpec(memory_space=pl.ANY)
    dma = pltpu.SemaphoreType.DMA
    return pl.pallas_call(
        kernel,
        out_shape=jax.ShapeDtypeStruct((tok, width), BF16),
        in_specs=[vmem, vmem, vmem, anywhere, anywhere, anywhere],
        out_specs=vmem,
        scratch_shapes=[
            pltpu.VMEM((width, 2 * ff), BF16),
            pltpu.VMEM((ff, width), BF16),
            pltpu.VMEM(cube + (tok, half + LANES), BF16),
            pltpu.VMEM((WAVES, 8, LANES, LANES), BF16),
            pltpu.VMEM((WAVES, 512, width), BF16),
            pltpu.VMEM((512, half), BF16),
            pltpu.VMEM((512, half), BF16),
            pltpu.VMEM((512, 2 * ff), F32),
            pltpu.VMEM((512, ff), BF16),
            pltpu.VMEM((WAVES, 512, half), BF16),
            pltpu.VMEM((tok, half), BF16),
            pltpu.VMEM((WAVES, 2, 2, SIDE, tok, half), BF16),
            pltpu.VMEM((WAVES, 2, SIDE, SIDE, tok, half), BF16),
            pltpu.VMEM((WAVES, 3, SIDE, tok, half), BF16),
            pltpu.VMEM((WAVES, 3, tok, half), BF16),
            dma((3,)),
            dma((72,)), dma((72,)),
            dma((3,)), dma((3,)),
            dma((4,)), dma((4,)),
            dma((4,)), dma((4,)),
            dma((72,)), dma((72,)),
        ],
        compiler_params=pltpu.CompilerParams(
            collective_id=0, has_side_effects=True, vmem_limit_bytes=VMEM_BYTES
        ),
        cost_estimate=pl.CostEstimate(flops=2 * 3 * 1024 * width * ff, bytes_accessed=6 * ff * width,
                                      transcendentals=1024 * ff),
    )(tokens, routes.T, router_weight.T, gate_weight[0], up_weight[0], down_weight[0])


def solution(mesh):
    in_specs = (
        P(("section", "expert"), None),
        P(("section", "expert"), None),
        P(),
        P("expert", None, "section"),
        P("expert", None, "section"),
        P("expert", "section", None),
    )
    out_specs = P(("section", "expert"), None)
    return jax.shard_map(shards, mesh=mesh, in_specs=in_specs, out_specs=out_specs, check_vma=False)
```
